256 devices in a mesh: dp: 8 (over z), ctx: 32 (over x, y, core).
Axes of the slice: x: 4, y: 4, z: 8, core: 2. Of those that a mesh axis runs over, the one named last changes fastest.
Arguments:
- conv_input: bfloat16 [8, 4096, 2816], P('dp', 'ctx'), may hold values from -6 to 6
- step_raw: float32 [8, 4096, 40], P('dp', 'ctx'), may hold values from -13 to -3
- log_decay: float32 [8, 4096, 40], P('dp', 'ctx'), may hold values from -1 to 0
- cotangent: bfloat16 [8, 4096, 2560], P('dp', 'ctx'), may hold values from -24 to 24
- conv_weight: float32 [4, 2816], replicated, may hold values from -3 to 3
- conv_bias: float32 [2816], replicated, may hold values from -0.5 to 0.5
- skip_gain: float32 [40], replicated, may hold values from 0.5 to 1.5
Outputs:
- layer_output: bfloat16 [8, 4096, 2560], P('dp', 'ctx')
- input_grad: bfloat16 [8, 4096, 2816], P('dp', 'ctx')
- step_grad: float32 [8, 4096, 40], P('dp', 'ctx')
- weight_grad: float32 [4, 2816], replicated
- bias_grad: float32 [2816], replicated
- skip_grad: float32 [40], replicated
The draws below stay inside these ranges and needn't reach their ends.
All inputs are finite; a program needn't handle non-finite values.
Results may differ from the reference program's by a relative error of at most 0.014.
Values may be sent and summed in bfloat16 or wider, within the bound.
A program may use at most 192 MiB of HBM per device.

```python
import math
import jax
import jax.numpy as jnp
from jax import lax

ATTENTION_LANES = 40
P_SIZE = 64
N = 128
K = 4
TOK_DEV = 128
SAMPLE_TOTAL = 8
SAMPLE_LENGTH = 4096
CH = 2816
N_CTX = 32


def draw_step_raw(key, part):
    key = jax.random.fold_in(key, 5)
    sizes_now = jnp.exp(jax.random.uniform(key, (SAMPLE_TOTAL, SAMPLE_LENGTH, ATTENTION_LANES), jnp.float32, math.log(0.2), math.log(2.0))) / SAMPLE_LENGTH
    return jnp.log(jnp.expm1(sizes_now))


def draw_log_decay(key, part):
    key = jax.random.fold_in(key, 11)
    prng_seed_list = jax.random.split(key, 7)
    fast_share = 0.5
    fast_heads = jax.random.bernoulli(prng_seed_list[0], fast_share, (SAMPLE_TOTAL, 1, ATTENTION_LANES))
    fast_rate = jax.random.uniform(prng_seed_list[1], (SAMPLE_TOTAL, 1, ATTENTION_LANES), jnp.float32, 0.02, 0.033)
    slow_rate = jnp.exp(jax.random.uniform(prng_seed_list[2], (SAMPLE_TOTAL, 1, ATTENTION_LANES), jnp.float32, math.log(0.1), math.log(0.4))) / SAMPLE_LENGTH
    default_decay_speed = jnp.where(fast_heads, fast_rate, slow_rate)
    block_count = SAMPLE_LENGTH // TOK_DEV
    segment_factor = jnp.exp(jax.random.uniform(prng_seed_list[3], (SAMPLE_TOTAL, block_count, 1, ATTENTION_LANES), jnp.float32, -math.log(2.0), math.log(2.0)))
    segment_factor = jnp.broadcast_to(segment_factor, (SAMPLE_TOTAL, block_count, TOK_DEV, ATTENTION_LANES)).reshape(SAMPLE_TOTAL, SAMPLE_LENGTH, ATTENTION_LANES)
    rough_scale_factor = jax.random.uniform(prng_seed_list[4], (SAMPLE_TOTAL, SAMPLE_LENGTH, ATTENTION_LANES), jnp.float32, 0.5, 1.5)
    step_indices = jax.random.randint(prng_seed_list[5], (SAMPLE_TOTAL, 3), 0, SAMPLE_LENGTH)
    spike_chosen_mask = jnp.any(jnp.arange(SAMPLE_LENGTH)[None, :, None] == step_indices[:, None, :], axis=2)
    spike_kept_mask = jax.random.uniform(prng_seed_list[6], (SAMPLE_TOTAL, SAMPLE_LENGTH, ATTENTION_LANES), jnp.float32, 0.5, 0.8)
    return -default_decay_speed * segment_factor * rough_scale_factor + jnp.where(spike_chosen_mask[:, :, None], jnp.log(spike_kept_mask), 0.0)


def draw_cotangent(key, part):
    key = jax.random.fold_in(key, 23)
    prng_seed_list = jax.random.split(key, 1)
    ramp = 1.0 + 2.0 * jnp.arange(SAMPLE_LENGTH, dtype=jnp.float32) / max(SAMPLE_LENGTH - 1, 1)
    seq_scale = 1.0 + jnp.arange(SAMPLE_TOTAL, dtype=jnp.float32) / max(SAMPLE_TOTAL - 1, 1)
    values = jax.random.normal(prng_seed_list[0], (SAMPLE_TOTAL, SAMPLE_LENGTH, ATTENTION_LANES * P_SIZE), jnp.float32)
    values = jnp.clip(values, -4.0, 4.0)
    return (values * ramp[None, :, None] * seq_scale[:, None, None]).astype(jnp.bfloat16)


def block_levels(key, shape, cuts, low, high):
    loudness, own = 1.0, jax.random.fold_in(key, 6)
    for position, blocks in cuts:
        heights = jnp.exp(jax.random.uniform(jax.random.fold_in(own, position), (blocks,), jnp.float32, low / len(cuts), high / len(cuts)))
        loudness = loudness * jnp.repeat(heights, shape[position] // blocks).reshape([-1 if axis == position else 1 for axis in range(len(shape))])
    return loudness


def gaussian(own_key, dims, width, bound, cuts=(), kind=jnp.bfloat16):
    result = width * jax.random.normal(own_key, dims, jnp.float32)
    if cuts:
        result = result * block_levels(own_key, dims, cuts, -0.22, 0.18)
    return jnp.clip(result, -bound, bound).astype(kind)


def setup_inputs(seed: int = 0) -> dict:
    seeds = jax.random.split(jax.random.key(seed), 8)
    return {
        "conv_input": gaussian(seeds[0], (SAMPLE_TOTAL, SAMPLE_LENGTH, CH), 1.0, 6.0, ((0, 8), (1, 32))),
        "step_raw": draw_step_raw(jax.random.fold_in(seeds[7], 71), 0),
        "log_decay": draw_log_decay(jax.random.fold_in(seeds[7], 71), 0),
        "cotangent": draw_cotangent(jax.random.fold_in(seeds[7], 71), 0),
        "conv_weight": gaussian(seeds[4], (K, CH), K ** -0.5, 3.0, (), jnp.float32),
        "conv_bias": jnp.clip(jax.random.uniform(seeds[5], (CH,), jnp.float32, -0.5, 0.5), -0.5, 0.5),
        "skip_gain": jnp.clip(jax.random.uniform(seeds[6], (ATTENTION_LANES,), jnp.float32, 0.5, 1.5), 0.5, 1.5),
    }


def conv_forward(series, conv_weight, conv_bias):
    length = series.shape[0]
    padded = jnp.concatenate([jnp.zeros((K - 1, series.shape[1]), jnp.float32), series.astype(jnp.float32)], axis=0)
    before = jnp.zeros((length, series.shape[1]), jnp.float32) + conv_bias[None, :]
    for offset in range(K):
        before = before + conv_weight[offset][None, :] * padded[offset:offset + length]
    return before, padded


def block_parts(act_block, raw_block, decay_block, cot_block):
    length = act_block.shape[0]
    signal = act_block[:, :ATTENTION_LANES * P_SIZE].reshape(length, ATTENTION_LANES, P_SIZE)
    inject = act_block[:, ATTENTION_LANES * P_SIZE:ATTENTION_LANES * P_SIZE + N]
    readout = act_block[:, ATTENTION_LANES * P_SIZE + N:]
    step_size = jax.nn.softplus(raw_block)
    decay_sum = jnp.cumsum(decay_block, axis=0)
    decay_end = decay_sum[length - 1]
    to_end = jnp.exp(decay_end[None, :] - decay_sum)
    from_start = jnp.exp(decay_sum)
    grad_heads = cot_block.reshape(length, ATTENTION_LANES, P_SIZE)
    signal_tail = (signal.astype(jnp.float32) * (step_size * to_end)[:, :, None]).astype(jnp.bfloat16)
    grad_start = (grad_heads.astype(jnp.float32) * from_start[:, :, None]).astype(jnp.bfloat16)
    return (signal, inject, readout, step_size, decay_sum, to_end, from_start, grad_heads,
            signal_tail, grad_start, jnp.exp(decay_end))


def block_local(blocks_in):
    parts = block_parts(*blocks_in)
    local_state = jnp.einsum('lhp,ln->hpn', parts[8].astype(jnp.float32), parts[1].astype(jnp.float32))
    local_adjoint = jnp.einsum('lhp,ln->hpn', parts[9].astype(jnp.float32), parts[2].astype(jnp.float32))
    return parts[10], local_state, local_adjoint


def block_finish(blocks_in, skip_gain):
    act_block, raw_block, decay_block, cot_block, incoming, adjoint = blocks_in
    parts = block_parts(act_block, raw_block, decay_block, cot_block)
    signal, inject, readout, step_size, decay_sum, to_end, from_start, grad_heads, signal_tail, grad_start = parts[:10]
    length = act_block.shape[0]
    scores = jnp.dot(readout, inject.T, preferred_element_type=jnp.float32)
    causal = jnp.arange(length)[:, None] >= jnp.arange(length)[None, :]
    sum_heads = decay_sum.T
    log_gap = jnp.where(causal[None], sum_heads[:, :, None] - sum_heads[:, None, :], -1e30)
    fading = jnp.exp(log_gap)
    mixing = (fading * scores[None]).astype(jnp.bfloat16)
    signal_step = (signal.astype(jnp.float32) * step_size[:, :, None]).astype(jnp.bfloat16)
    out_intra = jnp.einsum('hts,shp->thp', mixing.astype(jnp.float32), signal_step.astype(jnp.float32))
    back_intra = jnp.einsum('hts,thp->shp', mixing.astype(jnp.float32), grad_heads.astype(jnp.float32))
    inner_prod = jnp.einsum('thp,shp->hts', grad_heads.astype(jnp.float32), signal.astype(jnp.float32))
    mix_total = jnp.sum(fading * step_size.T[:, None, :] * inner_prod, axis=0).astype(jnp.bfloat16)
    incoming_b = incoming.astype(jnp.bfloat16).astype(jnp.float32)
    adjoint_b = adjoint.astype(jnp.bfloat16).astype(jnp.float32)
    out_full = (out_intra + from_start[:, :, None] * jnp.einsum('ln,hpn->lhp', readout.astype(jnp.float32), incoming_b)
                + skip_gain[None, :, None] * signal.astype(jnp.float32))
    back_full = back_intra + to_end[:, :, None] * jnp.einsum('ln,hpn->lhp', inject.astype(jnp.float32), adjoint_b)
    grad_signal = step_size[:, :, None] * back_full + skip_gain[None, :, None] * grad_heads.astype(jnp.float32)
    step_part = jnp.sum(signal.astype(jnp.float32) * back_full, axis=2) * jax.nn.sigmoid(raw_block)
    grad_readout = (jnp.dot(mix_total, inject, preferred_element_type=jnp.float32)
                    + jnp.einsum('lhp,hpn->ln', grad_start.astype(jnp.float32), incoming_b))
    grad_inject = (jnp.dot(mix_total.T, readout, preferred_element_type=jnp.float32)
                   + jnp.einsum('lhp,hpn->ln', signal_tail.astype(jnp.float32), adjoint_b))
    grad_act = jnp.concatenate([grad_signal.reshape(length, ATTENTION_LANES * P_SIZE), grad_inject, grad_readout], axis=1)
    skip_part = jnp.sum(grad_heads.astype(jnp.float32) * signal.astype(jnp.float32), axis=(0, 2))
    return out_full.reshape(length, ATTENTION_LANES * P_SIZE).astype(jnp.bfloat16), grad_act, step_part, skip_part


def reference(conv_input, step_raw, log_decay, cotangent, conv_weight, conv_bias, skip_gain):
    def forward_pass(carried, inputs_now):
        decay_now, state_now = inputs_now
        return decay_now[:, None, None] * carried + state_now, carried

    def one_sequence(sequence_in):
        series, raw_seq, decay_seq, cot_seq = sequence_in
        before, padded = conv_forward(series, conv_weight, conv_bias)
        activated = jax.nn.silu(before).astype(jnp.bfloat16)
        act_blocks = activated.reshape(N_CTX, TOK_DEV, CH)
        raw_blocks = raw_seq.reshape(N_CTX, TOK_DEV, ATTENTION_LANES)
        decay_blocks = decay_seq.reshape(N_CTX, TOK_DEV, ATTENTION_LANES)
        cot_blocks = cot_seq.reshape(N_CTX, TOK_DEV, ATTENTION_LANES * P_SIZE)
        block_decay, local_state, local_adjoint = lax.map(block_local, (act_blocks, raw_blocks, decay_blocks, cot_blocks))
        zero_state = jnp.zeros((ATTENTION_LANES, P_SIZE, N), jnp.float32)
        _, incoming = lax.scan(forward_pass, zero_state, (block_decay, local_state))
        _, adjoint = lax.scan(forward_pass, zero_state, (block_decay, local_adjoint), reverse=True)
        out_blocks, grad_blocks, step_blocks, skip_blocks = lax.map(
            lambda blocks_in: block_finish(blocks_in, skip_gain),
            (act_blocks, raw_blocks, decay_blocks, cot_blocks, incoming, adjoint))
        sigmoid_pre = jax.nn.sigmoid(before)
        grad_pre = grad_blocks.reshape(SAMPLE_LENGTH, CH) * sigmoid_pre * (1.0 + before * (1.0 - sigmoid_pre))
        padded_grad = jnp.concatenate([grad_pre, jnp.zeros((K - 1, CH), jnp.float32)], axis=0)
        grad_in = jnp.zeros((SAMPLE_LENGTH, CH), jnp.float32)
        for offset in range(K):
            grad_in = grad_in + conv_weight[offset][None, :] * padded_grad[K - 1 - offset:K - 1 - offset + SAMPLE_LENGTH]
        weight_part = jnp.stack([jnp.sum(grad_pre * padded[offset:offset + SAMPLE_LENGTH], axis=0) for offset in range(K)])
        bias_part = jnp.sum(grad_pre, axis=0)
        return (out_blocks.reshape(SAMPLE_LENGTH, ATTENTION_LANES * P_SIZE), grad_in.astype(jnp.bfloat16), step_blocks.reshape(SAMPLE_LENGTH, ATTENTION_LANES),
                weight_part, bias_part, jnp.sum(skip_blocks, axis=0))

    outs_all = lax.map(one_sequence, (conv_input, step_raw, log_decay, cotangent))
    return (outs_all[0], outs_all[1], outs_all[2], jnp.sum(outs_all[3], axis=0),
            jnp.sum(outs_all[4], axis=0), jnp.sum(outs_all[5], axis=0))
```

```python
import jax
import jax.numpy as jnp
from jax import lax
from jax.experimental import pallas as pl
from jax.experimental.pallas import tpu as pltpu
from jax.sharding import PartitionSpec as P

HEADS = 40
WIDTH = 64
STATE = 128
TAPS = 4
TOK = 128
SIG = HEADS * WIDTH
CH = SIG + 2 * STATE
BLOCKS = SIG // 128
CTX = 32
CHIPS = 16
DPS = 8
GROUPS = 4
GW = SIG // GROUPS
GB = GW // 128
HALF = STATE // 2
ROWS = 16
OWNERS = CH // 128
SPLIT = 10
LOG2E = 1.4426950408889634
F32 = jnp.float32
BF16 = jnp.bfloat16
MESH = pl.DeviceIdType.MESH


def dot(a, b, dims=((1,), (0,)), **kw):
    return lax.dot_general(a, b, (dims, ((), ())), preferred_element_type=F32, **kw)


def split3(v):
    hi = v.astype(BF16)
    rest = v - hi.astype(F32)
    mid = rest.astype(BF16)
    low = (rest - mid.astype(F32)).astype(BF16)
    return hi, mid, low


def loop(lo, hi, fn):
    def step(i, carry):
        fn(i)
        return carry

    lax.fori_loop(lo, hi, step, 0)


def cols(i, width=128):
    return pl.ds(pl.multiple_of(i * width, 128), width)


def kernel(
    x_ref, raw_ref, ld_ref, cot_ref, w_ref, b_ref, skip_ref,
    out_ref, gin_ref, sg_ref, wg_ref, bg_ref, kg_ref,
    xe, halo, act, dsil, ldp, dst, dsx, stx, fsx, tex, tail, gst, sst,
    loc, prt, dec, decp, decg, dcx, coef, skx, tsum, rcv, res, inc, snd, fin,
    oi, bi, run, gp, zhi, zlo, onehot, skp, part, ar1, ar2, sum1, tot,
    h_sem, d_sem, dg_s, dg_r, p1_s, p1_r, a_s, a_r, b_s, b_r, p2_s, p2_r, g_sem,
    r1_s, r1_r, r2_s, r2_r, r3_s, r3_r,
):
    me = lax.axis_index("ctx")
    zed = lax.axis_index("dp")
    core = lax.rem(me, 2)
    chip = me // 2
    quarter = lax.rem(chip, 4)
    band = chip // 4
    mate = me + 1 - 2 * core
    nxt = lax.rem(me + 1, CTX)
    prv = lax.rem(me + CTX - 1, CTX)

    def send(src, dst, ssem, rsem, ctx):
        return pltpu.make_async_remote_copy(
            src_ref=src, dst_ref=dst, send_sem=ssem, recv_sem=rsem,
            device_id={"ctx": ctx}, device_id_type=MESH,
        )

    barrier = pltpu.get_barrier_semaphore()

    def greet_ctx(i):
        pl.semaphore_signal(
            barrier, inc=1, device_id={"ctx": lax.rem(me + i, CTX)}, device_id_type=MESH
        )

    def greet_dp(i):
        pl.semaphore_signal(
            barrier, inc=1, device_id={"dp": lax.rem(zed + i, DPS)}, device_id_type=MESH
        )

    loop(1, CTX, greet_ctx)
    loop(1, DPS, greet_dp)

    rows = lax.broadcasted_iota(jnp.int32, (TOK, 128), 0)
    lanes = lax.broadcasted_iota(jnp.int32, (TOK, 128), 1)
    lower = rows >= lanes
    left = lanes < WIDTH

    ldp[...] = jnp.zeros((TOK, 128), F32)
    ldp[:, :HEADS] = ld_ref[...] * LOG2E
    sums = dot(lower.astype(F32), ldp[...], precision=lax.Precision.HIGHEST)
    dst[...] = sums.T
    decay = jnp.exp2(sums[TOK - 1 : TOK, :])
    dec[...] = jnp.broadcast_to(decay, (8, 128))
    xe[0:8, :] = jnp.zeros((8, CH), F32)

    pl.semaphore_wait(barrier, CTX - 1 + DPS - 1)

    halo_copy = send(x_ref.at[pl.ds(TOK - 16, 16), :], halo, h_sem.at[0], h_sem.at[1], nxt)
    halo_copy.start()
    decay_copy = send(dec, decp, d_sem.at[0], d_sem.at[1], mate)
    decay_copy.start()

    raw = raw_ref[...]
    steps = jnp.maximum(raw, 0.0) + jnp.log1p(jnp.exp(-jnp.abs(raw)))

    for h in range(HEADS):
        dsx[:, 128 * h : 128 * h + 128] = jnp.broadcast_to(sums[:, h : h + 1], (TOK, 128))
    for g in range(BLOCKS):
        c = slice(128 * g, 128 * g + 128)
        stx[:, c] = jnp.where(
            left,
            jnp.broadcast_to(steps[:, 2 * g : 2 * g + 1], (TOK, 128)),
            jnp.broadcast_to(steps[:, 2 * g + 1 : 2 * g + 2], (TOK, 128)),
        )
        onehot[c, :] = (lanes == 2 * g + (rows >= WIDTH).astype(jnp.int32)).astype(BF16)

    def expand(row, count):
        at = lax.broadcasted_iota(jnp.int32, (count, 128), 1) < WIDTH
        return [
            jnp.where(
                at,
                jnp.broadcast_to(row[:, 2 * g : 2 * g + 1], (count, 128)),
                jnp.broadcast_to(row[:, 2 * g + 1 : 2 * g + 2], (count, 128)),
            )
            for g in range(BLOCKS)
        ]

    for g, v in enumerate(expand(skip_ref[...], 1)):
        skx[:, 128 * g : 128 * g + 128] = v

    decay_copy.wait()
    mine, other = dec[0:1, :], decp[0:1, :]
    decg[chip] = dec[...] * decp[...]
    first = core == 0
    for g, (a, b) in enumerate(zip(expand(mine, 1), expand(other, 1))):
        c = slice(128 * g, 128 * g + 128)
        one = jnp.ones_like(a)
        coef[0:1, c] = jnp.where(first, b, one)
        coef[1:2, c] = jnp.where(first, one, a)
        coef[2:3, c] = jnp.where(first, one, b)
        coef[3:4, c] = jnp.where(first, a, one)
        coef[4:5, c] = a
        coef[5:6, c] = b

    def chip_at(i):
        return lax.rem(chip + i, CHIPS)

    def decay_out(q):
        return send(decg.at[chip], decg.at[chip], dg_s.at[q], dg_r.at[chip], 2 * q + core)

    def decay_in(q):
        return send(decg.at[q], decg.at[q], dg_s.at[q], dg_r.at[q], 2 * q + core)

    loop(1, CHIPS, lambda i: decay_out(chip_at(i)).start())

    xe[8:, :] = x_ref[...].astype(F32)
    halo_copy.wait()
    xe[0:8, :] = jnp.where(me > 0, halo[...].astype(F32)[8:16, :], 0.0)

    def conv(j):
        c = cols(j)
        pre = jnp.broadcast_to(b_ref[:, c], (TOK, 128))
        for k in range(TAPS):
            pre = pre + w_ref[k : k + 1, c] * xe[5 + k : 5 + k + TOK, c]
        sig = 1.0 / (1.0 + jnp.exp(-pre))
        act[:, c] = (pre * sig).astype(BF16)
        dsil[:, c] = sig * (1.0 + pre * (1.0 - sig))

    loop(0, CH // 128, conv)

    inject = act[:, SIG : SIG + STATE]
    readout = act[:, SIG + STATE :]
    inject_t = inject.T
    readout_t = readout.T

    def scaled(g):
        c = cols(g)
        ds = jnp.where(left, dsx[:, cols(2 * g)], dsx[:, cols(2 * g + 1)])
        start = jnp.exp2(ds)
        end = jnp.exp2(ds[TOK - 1 : TOK, :] - ds)
        fsx[:, c] = start
        tex[:, c] = end
        s = act[:, c].astype(F32)
        t = cot_ref[:, c].astype(F32)
        step = stx[:, c]
        tail[:, c] = (s * (step * end)).astype(BF16)
        sst[:, c] = (s * step).astype(BF16)
        gst[:, c] = (t * start).astype(BF16)
        skp[:, c] = jnp.sum((s * t).reshape(TOK // 8, 8, 128), axis=0)

    def pair_one(j):
        c = cols(j, GW)
        there = pl.ds(pl.multiple_of(HALF * (1 - core), HALF), HALF)
        return send(loc.at[:, there, c], prt.at[:, :, c], p1_s.at[j], p1_r.at[j], mate)

    def local_group(j):
        loop(0, GB, lambda i: scaled(j * GB + i))
        c = cols(j, GW)
        loc[0, :, c] = dot(inject_t, tail[:, c]).astype(BF16)
        loc[1, :, c] = dot(readout_t, gst[:, c]).astype(BF16)
        pair_one(j).start()

    loop(0, GROUPS, local_group)

    here = pl.ds(pl.multiple_of(HALF * core, HALF), HALF)

    def piece(ref, q):
        r = pl.ds(pl.multiple_of(ROWS * (q // 4), ROWS), ROWS)
        return ref.at[:, r, cols(lax.rem(q, 4), GW)]

    def state_out(q):
        return send(piece(tsum, q), rcv.at[chip], a_s.at[q], a_r.at[chip], 2 * q + core)

    def state_in(q):
        return send(piece(tsum, q), rcv.at[q], a_s.at[q], a_r.at[q], 2 * q + core)

    def chip_group(j):
        pair_one(j).wait_recv()
        c = cols(j, GW)
        tsum[0, :, c] = (
            coef[0:1, c] * loc[0, here, c].astype(F32) + coef[1:2, c] * prt[0, :, c].astype(F32)
        ).astype(BF16)
        tsum[1, :, c] = (
            coef[2:3, c] * loc[1, here, c].astype(F32) + coef[3:4, c] * prt[1, :, c].astype(F32)
        ).astype(BF16)

        def out(r):
            q = 4 * r + j

            @pl.when(q != chip)
            def _():
                state_out(q).start()

        loop(0, 4, out)

    loop(0, GROUPS, chip_group)
    own_piece = pl.ds(pl.multiple_of(ROWS * band, ROWS), ROWS)
    rcv[chip] = tsum[:, own_piece, cols(quarter, GW)]

    scores = dot(readout, inject, ((1,), (1,)))
    scores_t = dot(inject, readout, ((1,), (1,)))
    low_scores = jnp.where(lower, scores, 0.0)
    up_scores = jnp.where(rows <= lanes, scores_t, 0.0)
    run[...] = jnp.zeros((TOK, 128), F32)
    lane_a = left.astype(BF16)
    lane_b = (lanes >= WIDTH).astype(BF16)

    def intra(g):
        c = cols(g)
        fades = []
        for e in range(2):
            gap = dsx[:, cols(2 * g + e)] - dst[pl.ds(2 * g + e, 1), :]
            fades.append(jnp.exp2(jnp.where(lower, gap, -gap)))
        mix = jnp.concatenate([(f * low_scores).astype(BF16) for f in fades], axis=1)
        mix_t = jnp.concatenate([(f * up_scores).astype(BF16) for f in fades], axis=1)
        s = sst[:, c]
        t = cot_ref[:, c]
        both = jnp.concatenate([s * lane_a, s * lane_b], axis=0)
        oi[:, c] = dot(mix, both)
        bi[:, c] = dot(mix_t, jnp.concatenate([t * lane_a, t * lane_b], axis=0))
        inner = dot(t, both, ((1,), (1,)))
        run[...] += fades[0] * inner[:, :128] + fades[1] * inner[:, 128:]

    loop(0, SPLIT, intra)

    def decays_in(i):
        decay_in(chip_at(i)).wait_recv()

    loop(1, CHIPS, decays_in)
    all_decays = decg[:, 0, :]
    for g, v in enumerate(expand(all_decays, CHIPS)):
        dcx[:, 128 * g : 128 * g + 128] = v
    loop(1, CHIPS, lambda i: state_in(chip_at(i)).wait_recv())
    qc = cols(quarter, GW)

    def forward(q, carry):
        res[q, 0] = carry.astype(BF16)
        return dcx[pl.ds(q, 1), qc] * carry + rcv[q, 0].astype(F32)

    def backward(i, carry):
        q = CHIPS - 1 - i
        res[q, 1] = carry.astype(BF16)
        return dcx[pl.ds(q, 1), qc] * carry + rcv[q, 1].astype(F32)

    zero = jnp.zeros((ROWS, GW), F32)
    lax.fori_loop(0, CHIPS, forward, zero)
    lax.fori_loop(0, CHIPS, backward, zero)

    def result_out(q):
        return send(res.at[q], piece(inc, chip), b_s.at[q], b_r.at[chip], 2 * q + core)

    def result_in(q):
        return send(res.at[q], piece(inc, q), b_s.at[q], b_r.at[q], 2 * q + core)

    loop(1, CHIPS, lambda i: result_out(chip_at(i)).start())
    inc[:, own_piece, qc] = res[chip]

    loop(SPLIT, BLOCKS, intra)

    skip_rows = skp[...]
    skip_heads = sum(dot(v, onehot[...]) for v in split3(skip_rows))
    mix_total = jnp.where(lower, run[...], 0.0).astype(BF16)
    grad_readout = dot(mix_total, inject)
    grad_inject = dot(mix_total.T, readout)

    def pair_two(j):
        c = cols(j, GW)
        return send(snd.at[:, :, c], fin.at[:, here, c], p2_s.at[j], p2_r.at[j], mate)

    def spread_group(j):
        def arrive(r):
            q = 4 * r + j

            @pl.when(q != chip)
            def _():
                result_in(q).wait_recv()

        loop(0, 4, arrive)
        c = cols(j, GW)
        a, b = coef[4:5, c], coef[5:6, c]
        snd[core, :, c] = (
            a * inc[core, :, c].astype(F32) + loc[core, here, c].astype(F32)
        ).astype(BF16)
        snd[1 - core, :, c] = inc[1 - core, :, c]
        pair_two(j).start()
        fin[1 - core, here, c] = (
            b * inc[1 - core, :, c].astype(F32) + prt[1 - core, :, c].astype(F32)
        ).astype(BF16)
        fin[core, here, c] = inc[core, :, c]

    loop(0, GROUPS, spread_group)

    def finish_rows(c, grad_act):
        grad = grad_act * dsil[:, c]
        gp[0:TOK, c] = grad
        for k in range(TAPS):
            part[k : k + 1, c] = jnp.sum(grad * xe[5 + k : 5 + k + TOK, c], axis=0, keepdims=True)
        part[4:5, c] = jnp.sum(grad, axis=0, keepdims=True)

    def finish(g):
        c = cols(g)
        s = act[:, c].astype(F32)
        t = cot_ref[:, c].astype(F32)
        gain = skx[:, c]
        out = oi[:, c] + fsx[:, c] * dot(readout, fin[0, :, c]) + gain * s
        out_ref[:, c] = out.astype(BF16)
        back = bi[:, c] + tex[:, c] * dot(inject, fin[1, :, c])
        z = s * back
        z_hi = z.astype(BF16)
        zhi[:, c] = z_hi
        zlo[:, c] = (z - z_hi.astype(F32)).astype(BF16)
        finish_rows(c, stx[:, c] * back + gain * t)

    part[...] = jnp.zeros((8, CH), F32)
    part[5:6, 0:128] = jnp.sum(skip_heads, axis=0, keepdims=True)

    def finish_group(j):
        pair_two(j).wait_recv()
        loop(0, GB, lambda i: finish(j * GB + i))

    loop(0, GROUPS, finish_group)
    finish_rows(slice(SIG, SIG + STATE), grad_inject + dot(tail[...], fin[1], ((1,), (1,))))
    finish_rows(slice(SIG + STATE, CH), grad_readout + dot(gst[...], fin[0], ((1,), (1,))))

    def tile_out(j):
        return send(part.at[:, cols(j)], ar1.at[me], r1_s.at[j], r1_r.at[me], j)

    def tile_in(i):
        return send(part.at[:, cols(0)], ar1.at[i], r1_s.at[0], r1_r.at[i], i)

    def each_other(i, fn):
        @pl.when(i != me)
        def _():
            fn(i)

    loop(0, OWNERS, lambda j: each_other(j, lambda j: tile_out(j).start()))
    grad_halo = send(gp.at[pl.ds(0, 8), :], gp.at[pl.ds(TOK, 8), :], g_sem.at[0], g_sem.at[1], prv)
    grad_halo.start()

    steps_z = dot(zhi[...], onehot[...]) + dot(zlo[...], onehot[...])
    e = jnp.exp(-jnp.abs(raw))
    gate = jnp.where(raw >= 0, 1.0, e) / (1.0 + e)
    sg_ref[...] = steps_z[:, :HEADS] * gate

    def dp_out(i):
        z = lax.rem(zed + i, DPS)
        return pltpu.make_async_remote_copy(
            src_ref=sum1, dst_ref=ar2.at[zed], send_sem=r2_s.at[z], recv_sem=r2_r.at[zed],
            device_id={"dp": z}, device_id_type=MESH,
        )

    def dp_in(i):
        z = lax.rem(zed + i, DPS)
        return pltpu.make_async_remote_copy(
            src_ref=sum1, dst_ref=ar2.at[z], send_sem=r2_s.at[z], recv_sem=r2_r.at[z],
            device_id={"dp": z}, device_id_type=MESH,
        )

    def total_out(i):
        return send(tot.at[:, cols(me)], tot.at[:, cols(me)], r3_s.at[i], r3_r.at[me], i)

    def total_in(i):
        return send(tot.at[:, cols(i)], tot.at[:, cols(i)], r3_s.at[i], r3_r.at[i], i)

    owner = me < OWNERS

    @pl.when(owner)
    def _():
        loop(0, CTX, lambda i: each_other(i, lambda i: tile_in(i).wait_recv()))
        ar1[me] = part[:, cols(me)]
        sum1[...] = jnp.sum(ar1[...], axis=0)
        loop(1, DPS, lambda i: dp_out(i).start())

    grad_halo.wait_recv()
    gp[TOK:, :] = jnp.where(me < CTX - 1, gp[TOK:, :], 0.0)

    def input_grad(j):
        c = cols(j)
        total = w_ref[0:1, c] * gp[3 : 3 + TOK, c]
        for k in range(1, TAPS):
            total = total + w_ref[k : k + 1, c] * gp[3 - k : 3 - k + TOK, c]
        gin_ref[:, c] = total.astype(BF16)

    def reduce_dp():
        loop(1, DPS, lambda i: dp_in(i).wait_recv())
        ar2[zed] = sum1[...]
        tot[:, cols(me)] = jnp.sum(ar2[...], axis=0)
        loop(0, CTX, lambda i: each_other(i, lambda i: total_out(i).start()))

    pl.when(owner)(reduce_dp)

    loop(0, CH // 128, input_grad)

    loop(0, OWNERS, lambda i: each_other(i, lambda i: total_in(i).wait_recv()))
    wg_ref[...] = tot[0:TAPS, :]
    bg_ref[...] = tot[4:5, :]
    kg_ref[...] = tot[5:6, 0:HEADS]

    grad_halo.wait_send()
    loop(0, GROUPS, lambda j: (pair_one(j).wait_send(), pair_two(j).wait_send()) and None)

    def chips_done(i):
        q = chip_at(i)
        decay_out(q).wait_send()
        state_out(q).wait_send()
        result_out(q).wait_send()

    loop(1, CHIPS, chips_done)
    loop(0, OWNERS, lambda j: each_other(j, lambda j: tile_out(j).wait_send()))

    @pl.when(owner)
    def _():
        loop(1, DPS, lambda i: dp_out(i).wait_send())
        loop(0, CTX, lambda i: each_other(i, lambda i: total_out(i).wait_send()))


def scratch():
    v = pltpu.VMEM
    dma = pltpu.SemaphoreType.DMA
    return [
        v((TOK + 8, CH), F32),
        v((16, CH), BF16),
        v((TOK, CH), BF16),
        v((TOK, CH), F32),
        v((TOK, 128), F32),
        v((128, TOK), F32),
        v((TOK, HEADS * 128), F32),
        v((TOK, SIG), F32),
        v((TOK, SIG), F32),
        v((TOK, SIG), F32),
        v((TOK, SIG), BF16),
        v((TOK, SIG), BF16),
        v((TOK, SIG), BF16),
        v((2, STATE, SIG), BF16),
        v((2, HALF, SIG), BF16),
        v((8, 128), F32),
        v((8, 128), F32),
        v((CHIPS, 8, 128), F32),
        v((CHIPS, SIG), F32),
        v((8, SIG), F32),
        v((1, SIG), F32),
        v((2, HALF, SIG), BF16),
        v((CHIPS, 2, ROWS, GW), BF16),
        v((CHIPS, 2, ROWS, GW), BF16),
        v((2, HALF, SIG), BF16),
        v((2, HALF, SIG), BF16),
        v((2, STATE, SIG), BF16),
        v((TOK, SIG), F32),
        v((TOK, SIG), F32),
        v((TOK, 128), F32),
        v((TOK + 8, CH), F32),
        v((TOK, SIG), BF16),
        v((TOK, SIG), BF16),
        v((SIG, 128), BF16),
        v((8, SIG), F32),
        v((8, CH), F32),
        v((CTX, 8, 128), F32),
        v((DPS, 8, 128), F32),
        v((8, 128), F32),
        v((8, CH), F32),
        dma((2,)),
        dma((2,)),
        dma((CHIPS,)),
        dma((CHIPS,)),
        dma((GROUPS,)),
        dma((GROUPS,)),
        dma((CHIPS,)),
        dma((CHIPS,)),
        dma((CHIPS,)),
        dma((CHIPS,)),
        dma((GROUPS,)),
        dma((GROUPS,)),
        dma((2,)),
        dma((OWNERS,)),
        dma((CTX,)),
        dma((DPS,)),
        dma((DPS,)),
        dma((CTX,)),
        dma((CTX,)),
    ]


def body(conv_input, step_raw, log_decay, cotangent, conv_weight, conv_bias, skip_gain):
    vmem = pl.BlockSpec(memory_space=pltpu.VMEM)
    shapes = (
        jax.ShapeDtypeStruct((TOK, SIG), BF16),
        jax.ShapeDtypeStruct((TOK, CH), BF16),
        jax.ShapeDtypeStruct((TOK, HEADS), F32),
        jax.ShapeDtypeStruct((TAPS, CH), F32),
        jax.ShapeDtypeStruct((1, CH), F32),
        jax.ShapeDtypeStruct((1, HEADS), F32),
    )
    out, gin, sg, wg, bg, kg = pl.pallas_call(
        kernel,
        out_shape=shapes,
        in_specs=[vmem] * 7,
        out_specs=[vmem] * 6,
        scratch_shapes=scratch(),
        compiler_params=pltpu.CompilerParams(
            collective_id=0, has_side_effects=True, vmem_limit_bytes=52 * 1024 * 1024
        ),
    )(
        conv_input[0], step_raw[0], log_decay[0], cotangent[0],
        conv_weight, conv_bias[None], skip_gain[None],
    )
    return out[None], gin[None], sg[None], wg, bg[0], kg[0]


def solution(mesh):
    split = P("dp", "ctx", None)
    return jax.shard_map(
        body,
        mesh=mesh,
        in_specs=(split, split, split, split, P(), P(), P()),
        out_specs=(split, split, split, P(), P(), P()),
        check_vma=False,
    )
```

```python
import jax
import jax.numpy as jnp
from jax import lax
from jax.experimental import pallas as pl
from jax.experimental.pallas import tpu as pltpu
from jax.sharding import PartitionSpec as P

HEADS = 40
WIDTH = 64
STATE = 128
TAPS = 4
TOK = 128
SIG = HEADS * WIDTH
CH = SIG + 2 * STATE
BLOCKS = SIG // 128
CTX = 32
CHIPS = 16
DPS = 8
GROUPS = 4
GW = SIG // GROUPS
GB = GW // 128
HALF = STATE // 2
ROWS = 16
OWNERS = CH // 128
SPLIT_A = 6
SPLIT_B = 13
VMEM = 60 * 1024 * 1024
LOG2E = 1.4426950408889634
F32 = jnp.float32
BF16 = jnp.bfloat16
MESH = pl.DeviceIdType.MESH


def dot(a, b, dims=((1,), (0,)), **kw):
    return lax.dot_general(a, b, (dims, ((), ())), preferred_element_type=F32, **kw)


def split3(v):
    hi = v.astype(BF16)
    rest = v - hi.astype(F32)
    mid = rest.astype(BF16)
    low = (rest - mid.astype(F32)).astype(BF16)
    return hi, mid, low


def loop(lo, hi, fn):
    def step(i, carry):
        fn(i)
        return carry

    lax.fori_loop(lo, hi, step, 0)


def cols(i, width=128):
    return pl.ds(pl.multiple_of(i * width, 128), width)


def kernel(
    x_hbm, raw_hbm, ld_hbm, cot_hbm, w_hbm, b_hbm, skip_hbm,
    out_hbm, gin_hbm, sg_ref, wg_ref, bg_ref, kg_ref,
    out_ref, gin_ref, xb, cot_ref, w_ref, b_ref, skip_ref, raw_ref,
    xe, halo, act, dsil, ldp, stp, dst, dsx, stx, fsx, tex, tail, gst, sst,
    loc, prt, dec, decp, decg, dcx, coef, skx, tsum, rcv, res, inc, snd, fin,
    oi, bi, run, gp, zhi, zlo, onehot, skp, part, ar1, ar2, sum1, tot,
    in_sem, o_sem, h_sem, d_sem, dg_s, dg_r, p1_s, p1_r, a_s, a_r, b_s, b_r, p2_s, p2_r, g_sem,
    r1_s, r1_r, r2_s, r2_r, r3_s, r3_r,
):
    me = lax.axis_index("ctx")
    zed = lax.axis_index("dp")
    core = lax.rem(me, 2)
    chip = me // 2
    quarter = lax.rem(chip, 4)
    band = chip // 4
    mate = me + 1 - 2 * core
    nxt = lax.rem(me + 1, CTX)
    prv = lax.rem(me + CTX - 1, CTX)
    first = core == 0

    def send(src, dst, ssem, rsem, ctx):
        return pltpu.make_async_remote_copy(
            src_ref=src, dst_ref=dst, send_sem=ssem, recv_sem=rsem,
            device_id={"ctx": ctx}, device_id_type=MESH,
        )

    barrier = pltpu.get_barrier_semaphore()

    def greet_ctx(i):
        pl.semaphore_signal(
            barrier, inc=1, device_id={"ctx": lax.rem(me + i, CTX)}, device_id_type=MESH
        )

    def greet_dp(i):
        pl.semaphore_signal(
            barrier, inc=1, device_id={"dp": lax.rem(zed + i, DPS)}, device_id_type=MESH
        )

    fetch = [
        pltpu.make_async_copy(src, dst, in_sem.at[i])
        for i, (src, dst) in enumerate((
            (ld_hbm, ldp.at[pl.ds(0, HEADS), :]), (raw_hbm, raw_ref), (x_hbm, xb), (cot_hbm, cot_ref),
            (w_hbm, w_ref), (b_hbm, b_ref), (skip_hbm, skip_ref),
        ))
    ]
    for copy in fetch:
        copy.start()
    loop(1, CTX, greet_ctx)
    loop(1, DPS, greet_dp)

    rows = lax.broadcasted_iota(jnp.int32, (TOK, 128), 0)
    lanes = lax.broadcasted_iota(jnp.int32, (TOK, 128), 1)
    lower = rows >= lanes
    left = lanes < WIDTH

    ldp[HEADS:, :] = jnp.zeros((128 - HEADS, TOK), F32)
    stp[...] = jnp.zeros((128, TOK), F32)
    xe[0:8, :] = jnp.zeros((8, CH), F32)
    for copy in fetch:
        copy.wait()

    sums_t = dot(ldp[...] * LOG2E, (rows <= lanes).astype(F32), precision=lax.Precision.HIGHEST)
    dst[...] = sums_t
    sums = sums_t.T
    decay = jnp.exp2(sums[TOK - 1 : TOK, :])
    dec[...] = jnp.broadcast_to(decay, (8, 128))
    raw = raw_ref[...]
    stp[0:HEADS, :] = jnp.maximum(raw, 0.0) + jnp.log1p(jnp.exp(-jnp.abs(raw)))
    steps = stp[...].T

    for h in range(HEADS):
        dsx[:, 128 * h : 128 * h + 128] = jnp.broadcast_to(sums[:, h : h + 1], (TOK, 128))
    for g in range(BLOCKS):
        c = slice(128 * g, 128 * g + 128)
        stx[:, c] = jnp.where(
            left,
            jnp.broadcast_to(steps[:, 2 * g : 2 * g + 1], (TOK, 128)),
            jnp.broadcast_to(steps[:, 2 * g + 1 : 2 * g + 2], (TOK, 128)),
        )
        onehot[c, :] = (lanes == 2 * g + (rows >= WIDTH).astype(jnp.int32)).astype(BF16)

    def expand(row, count):
        at = lax.broadcasted_iota(jnp.int32, (count, 128), 1) < WIDTH
        return [
            jnp.where(
                at,
                jnp.broadcast_to(row[:, 2 * g : 2 * g + 1], (count, 128)),
                jnp.broadcast_to(row[:, 2 * g + 1 : 2 * g + 2], (count, 128)),
            )
            for g in range(BLOCKS)
        ]

    for g, v in enumerate(expand(skip_ref[...], 1)):
        skx[:, 128 * g : 128 * g + 128] = v

    def conv(j, r0, n):
        c = cols(j)
        pre = jnp.broadcast_to(b_ref[pl.ds(j, 1), :], (n, 128))
        for k in range(TAPS):
            pre = pre + w_ref[k : k + 1, c] * xe[5 + k + r0 : 5 + k + r0 + n, c]
        sig = 1.0 / (1.0 + jnp.exp(-pre))
        act[r0 : r0 + n, c] = (pre * sig).astype(BF16)
        dsil[r0 : r0 + n, c] = sig * (1.0 + pre * (1.0 - sig))

    def starts(g):
        c = cols(g)
        ds = jnp.where(left, dsx[:, cols(2 * g)], dsx[:, cols(2 * g + 1)])
        start = jnp.exp2(ds)
        fsx[:, c] = start
        tex[:, c] = jnp.exp2(ds[TOK - 1 : TOK, :] - ds)
        gst[:, c] = (cot_ref[:, c].astype(F32) * start).astype(BF16)

    def scaled(g, r0, n):
        c = cols(g)
        r = slice(r0, r0 + n)
        s = act[r, c].astype(F32)
        step = stx[r, c]
        tail[r, c] = (s * (step * tex[r, c])).astype(BF16)
        sst[r, c] = (s * step).astype(BF16)

    def later_rows(j):
        c = cols(j)
        xe[8:, c] = xb[:, c].astype(F32)
        conv(j, ROWS, TOK - ROWS)

    def later_signal(g):
        later_rows(g)
        starts(g)
        scaled(g, ROWS, TOK - ROWS)

    loop(0, BLOCKS, later_signal)
    loop(BLOCKS, BLOCKS + 2, later_rows)

    pl.semaphore_wait(barrier, CTX - 1 + DPS - 1)

    halo_copy = send(xb.at[pl.ds(TOK - 16, 16), :], halo, h_sem.at[0], h_sem.at[1], nxt)
    halo_copy.start()
    decay_copy = send(dec, decp, d_sem.at[0], d_sem.at[1], mate)
    decay_copy.start()

    decay_copy.wait()
    mine, other = dec[0:1, :], decp[0:1, :]
    decg[chip] = dec[...] * decp[...]

    def chip_at(i):
        return lax.rem(chip + i, CHIPS)

    def decay_out(q):
        return send(decg.at[chip], decg.at[chip], dg_s.at[q], dg_r.at[chip], 2 * q + core)

    def decay_in(q):
        return send(decg.at[q], decg.at[q], dg_s.at[q], dg_r.at[q], 2 * q + core)

    loop(1, CHIPS, lambda i: decay_out(chip_at(i)).start())
    for g, (a, b) in enumerate(zip(expand(mine, 1), expand(other, 1))):
        c = slice(128 * g, 128 * g + 128)
        coef[0:1, c] = a
        coef[1:2, c] = b

    halo_copy.wait_recv()
    xe[0:8, :] = jnp.where(me > 0, halo[...].astype(F32)[8:16, :], 0.0)
    loop(BLOCKS, BLOCKS + 2, lambda j: conv(j, 0, ROWS))
    inject = act[:, SIG : SIG + STATE]
    readout = act[:, SIG + STATE :]

    def pair_one(k, j):
        c = cols(j, GW)
        there = pl.ds(pl.multiple_of(HALF * (1 - core), HALF), HALF)
        return send(loc.at[k, there, c], prt.at[k, :, c], p1_s.at[k, j], p1_r.at[k, j], mate)

    readout_t = readout.T

    def local_adjoint(j):
        c = cols(j, GW)
        loc[1, :, c] = dot(readout_t, gst[:, c]).astype(BF16)
        pair_one(1, j).start()

    loop(0, GROUPS, local_adjoint)

    def early_rows(g):
        conv(g, 0, ROWS)
        scaled(g, 0, ROWS)

    loop(0, BLOCKS, early_rows)
    inject_t = inject.T

    def local_state(j):
        c = cols(j, GW)
        loc[0, :, c] = dot(inject_t, tail[:, c]).astype(BF16)
        pair_one(0, j).start()

    here = pl.ds(pl.multiple_of(HALF * core, HALF), HALF)
    own_rows = pl.ds(pl.multiple_of(ROWS * band, ROWS), ROWS)
    qc = cols(quarter, GW)

    def piece(ref, k, q):
        r = pl.ds(pl.multiple_of(ROWS * (q // 4), ROWS), ROWS)
        return ref.at[k, r, cols(lax.rem(q, 4), GW)]

    def state_out(k, q):
        return send(
            piece(tsum, k, q), rcv.at[k, chip], a_s.at[k, q], a_r.at[k, chip], 2 * q + core
        )

    def state_in(k, q):
        return send(piece(tsum, k, q), rcv.at[k, q], a_s.at[k, q], a_r.at[k, q], 2 * q + core)

    def chip_sums(k):
        def group(j):
            pair_one(k, j).wait_recv()
            c = cols(j, GW)
            a, b = coef[0:1, c], coef[1:2, c]
            own = loc[k, here, c].astype(F32)
            far = prt[k, :, c].astype(F32)
            if k == 0:
                total = jnp.where(first, b * own + far, a * far + own)
            else:
                total = jnp.where(first, a * far + own, b * own + far)
            tsum[k, :, c] = total.astype(BF16)

            def out(r):
                q = 4 * r + j

                @pl.when(q != chip)
                def _():
                    state_out(k, q).start()

            loop(0, 4, out)

        loop(0, GROUPS, group)
        rcv[k, chip] = tsum[k, own_rows, qc]

    chip_sums(1)
    loop(0, GROUPS, local_state)
    chip_sums(0)

    scores = dot(readout, inject, ((1,), (1,)))
    scores_t = dot(inject, readout, ((1,), (1,)))
    low_scores = jnp.where(lower, scores, 0.0)
    up_scores = jnp.where(rows <= lanes, scores_t, 0.0)
    run[...] = jnp.zeros((TOK, 128), F32)
    lane_a = left.astype(BF16)
    lane_b = (lanes >= WIDTH).astype(BF16)

    def intra(g):
        c = cols(g)
        fades = []
        for e in range(2):
            gap = dsx[:, cols(2 * g + e)] - dst[pl.ds(2 * g + e, 1), :]
            fades.append(jnp.exp2(jnp.where(lower, gap, -gap)))
        mix = jnp.concatenate([(f * low_scores).astype(BF16) for f in fades], axis=1)
        mix_t = jnp.concatenate([(f * up_scores).astype(BF16) for f in fades], axis=1)
        s = sst[:, c]
        t = cot_ref[:, c]
        both = jnp.concatenate([s * lane_a, s * lane_b], axis=0)
        oi[:, c] = dot(mix, both)
        bi[:, c] = dot(mix_t, jnp.concatenate([t * lane_a, t * lane_b], axis=0))
        inner = dot(t, both, ((1,), (1,)))
        run[...] += fades[0] * inner[:, :128] + fades[1] * inner[:, 128:]
        skp[:, c] = jnp.sum((act[:, c].astype(F32) * t.astype(F32)).reshape(TOK // 8, 8, 128), axis=0)

    loop(0, SPLIT_A, intra)

    loop(1, CHIPS, lambda i: decay_in(chip_at(i)).wait_recv())
    for g, v in enumerate(expand(decg[:, 0, :], CHIPS)):
        dcx[:, 128 * g : 128 * g + 128] = v

    def result_out(k, q):
        return send(res.at[k, q], piece(inc, k, chip), b_s.at[k, q], b_r.at[k, chip], 2 * q + core)

    def result_in(k, q):
        return send(res.at[k, q], piece(inc, k, q), b_s.at[k, q], b_r.at[k, q], 2 * q + core)

    def scan(k):
        loop(1, CHIPS, lambda i: state_in(k, chip_at(i)).wait_recv())

        def step(i, carry):
            q = i if k == 0 else CHIPS - 1 - i
            res[k, q] = carry.astype(BF16)
            return dcx[pl.ds(q, 1), qc] * carry + rcv[k, q].astype(F32)

        lax.fori_loop(0, CHIPS, step, jnp.zeros((ROWS, GW), F32))
        loop(1, CHIPS, lambda i: result_out(k, chip_at(i)).start())
        inc[k, own_rows, qc] = res[k, chip]

    scan(1)
    loop(SPLIT_A, SPLIT_B, intra)
    scan(0)
    loop(SPLIT_B, BLOCKS, intra)

    skip_heads = sum(dot(v, onehot[...]) for v in split3(skp[...]))
    mix_total = jnp.where(lower, run[...], 0.0).astype(BF16)
    grad_readout = dot(mix_total, inject)
    grad_inject = dot(mix_total.T, readout)
    part[...] = jnp.zeros((8, CH), F32)
    part[5:6, 0:128] = jnp.sum(skip_heads, axis=0, keepdims=True)

    def pair_two(k, j):
        c = cols(j, GW)
        return send(snd.at[k, :, c], fin.at[k, here, c], p2_s.at[k, j], p2_r.at[k, j], mate)

    def spread(k):
        def group(j):
            def arrive(r):
                q = 4 * r + j

                @pl.when(q != chip)
                def _():
                    result_in(k, q).wait_recv()

            loop(0, 4, arrive)
            c = cols(j, GW)
            came = inc[k, :, c]
            wide = came.astype(F32)
            near = (coef[0:1, c] * wide + loc[k, here, c].astype(F32)).astype(BF16)
            far = (coef[1:2, c] * wide + prt[k, :, c].astype(F32)).astype(BF16)
            if k == 0:
                snd[k, :, c] = jnp.where(first, near, came)
                fin[k, here, c] = jnp.where(first, came, far)
            else:
                snd[k, :, c] = jnp.where(first, came, near)
                fin[k, here, c] = jnp.where(first, far, came)
            pair_two(k, j).start()

        loop(0, GROUPS, group)

    spread(1)

    def tile_out(j):
        return send(part.at[:, cols(j)], ar1.at[me], r1_s.at[j], r1_r.at[me], j)

    def tile_in(i):
        return send(part.at[:, cols(0)], ar1.at[i], r1_s.at[0], r1_r.at[i], i)

    def each_other(i, fn):
        @pl.when(i != me)
        def _():
            fn(i)

    def finish_rows(j, grad_act):
        c = cols(j)
        grad = grad_act * dsil[:, c]
        gp[0:TOK, c] = grad
        for k in range(TAPS):
            part[k : k + 1, c] = jnp.sum(grad * xe[5 + k : 5 + k + TOK, c], axis=0, keepdims=True)
        part[4:5, c] = jnp.sum(grad, axis=0, keepdims=True)
        each_other(j, lambda j: tile_out(j).start())

    def finish(g):
        c = cols(g)
        s = act[:, c].astype(F32)
        t = cot_ref[:, c].astype(F32)
        back = bi[:, c] + tex[:, c] * dot(inject, fin[1, :, c])
        z = s * back
        z_hi = z.astype(BF16)
        zhi[:, c] = z_hi
        zlo[:, c] = (z - z_hi.astype(F32)).astype(BF16)
        finish_rows(g, stx[:, c] * back + skx[:, c] * t)

    def finish_group(j):
        pair_two(1, j).wait_recv()
        loop(0, GB, lambda i: finish(j * GB + i))

    loop(0, GROUPS, finish_group)
    finish_rows(BLOCKS, grad_inject + dot(tail[...], fin[1], ((1,), (1,))))
    spread(0)
    loop(0, GROUPS, lambda j: pair_two(0, j).wait_recv())
    finish_rows(BLOCKS + 1, grad_readout + dot(gst[...], fin[0], ((1,), (1,))))

    grad_halo = send(gp.at[pl.ds(0, 8), :], gp.at[pl.ds(TOK, 8), :], g_sem.at[0], g_sem.at[1], prv)
    grad_halo.start()

    def output(g):
        c = cols(g)
        out = oi[:, c] + fsx[:, c] * dot(readout, fin[0, :, c]) + skx[:, c] * act[:, c].astype(F32)
        out_ref[:, c] = out.astype(BF16)

    loop(0, BLOCKS, output)
    out_copy = pltpu.make_async_copy(out_ref, out_hbm, o_sem.at[0])
    out_copy.start()

    def dp_out(i):
        z = lax.rem(zed + i, DPS)
        return pltpu.make_async_remote_copy(
            src_ref=sum1, dst_ref=ar2.at[zed], send_sem=r2_s.at[z], recv_sem=r2_r.at[zed],
            device_id={"dp": z}, device_id_type=MESH,
        )

    def dp_in(i):
        z = lax.rem(zed + i, DPS)
        return pltpu.make_async_remote_copy(
            src_ref=sum1, dst_ref=ar2.at[z], send_sem=r2_s.at[z], recv_sem=r2_r.at[z],
            device_id={"dp": z}, device_id_type=MESH,
        )

    def total_out(i):
        return send(tot.at[:, cols(me)], tot.at[:, cols(me)], r3_s.at[i], r3_r.at[me], i)

    def total_in(i):
        return send(tot.at[:, cols(i)], tot.at[:, cols(i)], r3_s.at[i], r3_r.at[i], i)

    owner = me < OWNERS

    @pl.when(owner)
    def _():
        loop(0, CTX, lambda i: each_other(i, lambda i: tile_in(i).wait_recv()))
        ar1[me] = part[:, cols(me)]
        sum1[...] = jnp.sum(ar1[...], axis=0)
        loop(1, DPS, lambda i: dp_out(i).start())

    steps_z = dot(zhi[...], onehot[...]) + dot(zlo[...], onehot[...])
    e = jnp.exp(-jnp.abs(raw))
    gate = jnp.where(raw >= 0, 1.0, e) / (1.0 + e)
    sg_ref[...] = steps_z.T[0:HEADS, :] * gate

    grad_halo.wait_recv()
    gp[TOK:, :] = jnp.where(me < CTX - 1, gp[TOK:, :], 0.0)

    def input_grad(j):
        c = cols(j)
        total = w_ref[0:1, c] * gp[3 : 3 + TOK, c]
        for k in range(1, TAPS):
            total = total + w_ref[k : k + 1, c] * gp[3 - k : 3 - k + TOK, c]
        gin_ref[:, c] = total.astype(BF16)

    loop(0, CH // 256, input_grad)

    @pl.when(owner)
    def _():
        loop(1, DPS, lambda i: dp_in(i).wait_recv())
        ar2[zed] = sum1[...]
        tot[:, cols(me)] = jnp.sum(ar2[...], axis=0)
        loop(0, CTX, lambda i: each_other(i, lambda i: total_out(i).start()))

    loop(CH // 256, CH // 128, input_grad)
    gin_copy = pltpu.make_async_copy(gin_ref, gin_hbm, o_sem.at[1])
    gin_copy.start()

    halo_copy.wait_send()
    grad_halo.wait_send()

    def pairs_done(j):
        for k in range(2):
            pair_one(k, j).wait_send()
            pair_two(k, j).wait_send()

    def chips_done(i):
        q = chip_at(i)
        decay_out(q).wait_send()
        for k in range(2):
            state_out(k, q).wait_send()
            result_out(k, q).wait_send()

    loop(0, GROUPS, pairs_done)
    loop(1, CHIPS, chips_done)
    loop(0, OWNERS, lambda j: each_other(j, lambda j: tile_out(j).wait_send()))

    loop(0, OWNERS, lambda i: each_other(i, lambda i: total_in(i).wait_recv()))
    wg_ref[...] = tot[0:TAPS, :]
    for j in range(OWNERS):
        bg_ref[j : j + 1, :] = tot[4:5, 128 * j : 128 * j + 128]
    kg_ref[...] = tot[5:6, 0:HEADS]
    out_copy.wait()
    gin_copy.wait()

    @pl.when(owner)
    def _():
        loop(1, DPS, lambda i: dp_out(i).wait_send())
        loop(0, CTX, lambda i: each_other(i, lambda i: total_out(i).wait_send()))


def copy_kernel(*refs):
    n = (len(refs) - 1) // 2
    sem = refs[-1]
    copies = [
        pltpu.make_async_copy(refs[i], refs[n + i], sem.at[i]) for i in range(n)
    ]
    for copy in copies:
        copy.start()
    for copy in copies:
        copy.wait()


def scratch():
    v = pltpu.VMEM
    dma = pltpu.SemaphoreType.DMA
    return [
        v((TOK, SIG), BF16),
        v((TOK, CH), BF16),
        v((TOK, CH), BF16),
        v((TOK, SIG), BF16),
        v((TAPS, CH), F32),
        v((OWNERS, 128), F32),
        v((1, HEADS), F32),
        v((HEADS, TOK), F32),
        v((TOK + 8, CH), F32),
        v((16, CH), BF16),
        v((TOK, CH), BF16),
        v((TOK, CH), F32),
        v((128, TOK), F32),
        v((128, TOK), F32),
        v((128, TOK), F32),
        v((TOK, HEADS * 128), F32),
        v((TOK, SIG), F32),
        v((TOK, SIG), F32),
        v((TOK, SIG), F32),
        v((TOK, SIG), BF16),
        v((TOK, SIG), BF16),
        v((TOK, SIG), BF16),
        v((2, STATE, SIG), BF16),
        v((2, HALF, SIG), BF16),
        v((8, 128), F32),
        v((8, 128), F32),
        v((CHIPS, 8, 128), F32),
        v((CHIPS, SIG), F32),
        v((8, SIG), F32),
        v((1, SIG), F32),
        v((2, HALF, SIG), BF16),
        v((2, CHIPS, ROWS, GW), BF16),
        v((2, CHIPS, ROWS, GW), BF16),
        v((2, HALF, SIG), BF16),
        v((2, HALF, SIG), BF16),
        v((2, STATE, SIG), BF16),
        v((TOK, SIG), F32),
        v((TOK, SIG), F32),
        v((TOK, 128), F32),
        v((TOK + 8, CH), F32),
        v((TOK, SIG), BF16),
        v((TOK, SIG), BF16),
        v((SIG, 128), BF16),
        v((8, SIG), F32),
        v((8, CH), F32),
        v((CTX, 8, 128), F32),
        v((DPS, 8, 128), F32),
        v((8, 128), F32),
        v((8, CH), F32),
        dma((7,)),
        dma((2,)),
        dma((2,)),
        dma((2,)),
        dma((CHIPS,)),
        dma((CHIPS,)),
        dma((2, GROUPS)),
        dma((2, GROUPS)),
        dma((2, CHIPS)),
        dma((2, CHIPS)),
        dma((2, CHIPS)),
        dma((2, CHIPS)),
        dma((2, GROUPS)),
        dma((2, GROUPS)),
        dma((2,)),
        dma((OWNERS,)),
        dma((CTX,)),
        dma((DPS,)),
        dma((DPS,)),
        dma((CTX,)),
        dma((CTX,)),
    ]


def body(conv_input, step_raw, log_decay, cotangent, conv_weight, conv_bias, skip_gain):
    vmem = pl.BlockSpec(memory_space=pltpu.VMEM)
    hbm = pl.BlockSpec(memory_space=pltpu.HBM)
    shapes = (
        jax.ShapeDtypeStruct((TOK, SIG), BF16),
        jax.ShapeDtypeStruct((TOK, CH), BF16),
        jax.ShapeDtypeStruct((HEADS, TOK), F32),
        jax.ShapeDtypeStruct((TAPS, CH), F32),
        jax.ShapeDtypeStruct((OWNERS, 128), F32),
        jax.ShapeDtypeStruct((1, HEADS), F32),
    )
    results = pl.pallas_call(
        kernel,
        out_shape=shapes,
        in_specs=[hbm] * 7,
        out_specs=[hbm] * 2 + [vmem] * 4,
        scratch_shapes=scratch(),
        compiler_params=pltpu.CompilerParams(
            collective_id=0, has_side_effects=True, vmem_limit_bytes=VMEM
        ),
    )(
        conv_input[0], step_raw[0].T, log_decay[0].T, cotangent[0],
        conv_weight, conv_bias.reshape(OWNERS, 128), skip_gain[None],
    )
    out, gin, sg, wg, bg, kg = pl.pallas_call(
        copy_kernel,
        out_shape=shapes,
        in_specs=[vmem] * 6,
        out_specs=[hbm] * 6,
        scratch_shapes=[pltpu.SemaphoreType.DMA((6,))],
    )(*results)
    return out[None], gin[None], sg.T[None], wg, bg.reshape(CH), kg[0]


def solution(mesh):
    split = P("dp", "ctx", None)
    return jax.shard_map(
        body,
        mesh=mesh,
        in_specs=(split, split, split, split, P(), P(), P()),
        out_specs=(split, split, split, P(), P(), P()),
        check_vma=False,
    )
```

```python
import jax
import jax.numpy as jnp
from jax import lax
from jax.experimental import pallas as pl
from jax.experimental.pallas import tpu as pltpu
from jax.sharding import PartitionSpec as P

HEADS = 40
WIDTH = 64
STATE = 128
TAPS = 4
TOK = 128
SIG = HEADS * WIDTH
CH = SIG + 2 * STATE
BLOCKS = SIG // 128
CTX = 32
CHIPS = 16
DPS = 8
GROUPS = 4
GW = SIG // GROUPS
GB = GW // 128
HALF = STATE // 2
ROWS = 16
OWNERS = CH // 128
CUT_HALO = 6
CUT_PAIR = 12
CUT_SUMS = 3
CUT_BACK = 8
CUT_AHEAD = 14
VMEM = 60 * 1024 * 1024
LOG2E = 1.4426950408889634
F32 = jnp.float32
BF16 = jnp.bfloat16
MESH = pl.DeviceIdType.MESH


def dot(a, b, dims=((1,), (0,)), **kw):
    return lax.dot_general(a, b, (dims, ((), ())), preferred_element_type=F32, **kw)


def split3(v):
    hi = v.astype(BF16)
    rest = v - hi.astype(F32)
    mid = rest.astype(BF16)
    low = (rest - mid.astype(F32)).astype(BF16)
    return hi, mid, low


def loop(lo, hi, fn, unroll=1):
    whole = lo + (hi - lo) // unroll * unroll

    def step(i, carry):
        for k in range(unroll):
            fn(lo + i * unroll + k)
        return carry

    if whole > lo:
        lax.fori_loop(0, (whole - lo) // unroll, step, 0)
    for i in range(whole, hi):
        fn(jnp.int32(i))


def cols(i, width=128):
    return pl.ds(pl.multiple_of(i * width, 128), width)


def kernel(
    x_hbm, raw_hbm, ld_hbm, cot_hbm, w_hbm, b_hbm, skip_hbm,
    out_hbm, gin_hbm, sg_ref, wg_ref, bg_ref, kg_ref,
    out_ref, gin_ref, xb, cot_ref, w_ref, b_ref, skip_ref, raw_ref,
    xe, halo, act, dsil, ldp, stp, dst, dsx, stx, fsx, tex, tail, gst, sst,
    loc, prt, dec, decp, decg, dcx, coef, skx, tsum, rcv, res, inc, snd, fin,
    oi, bi, run, tmp, xsh, gp, zhi, zlo, onehot, skp, part, ar1, ar2, sum1, tot,
    in_sem, o_sem, h_sem, d_sem, dg_s, p1_s, p1_r, a_s, a_r, b_s, b_r, p2_s, p2_r, g_sem,
    r1_s, r2_s, r3_s,
):
    me = lax.axis_index("ctx")
    zed = lax.axis_index("dp")
    core = lax.rem(me, 2)
    chip = me // 2
    quarter = lax.rem(chip, 4)
    band = chip // 4
    mate = me + 1 - 2 * core
    nxt = lax.rem(me + 1, CTX)
    prv = lax.rem(me + CTX - 1, CTX)
    first = core == 0

    def send(src, dst, ssem, rsem, ctx):
        return pltpu.make_async_remote_copy(
            src_ref=src, dst_ref=dst, send_sem=ssem, recv_sem=rsem,
            device_id={"ctx": ctx}, device_id_type=MESH,
        )

    def left_all(ref, sem):
        send(ref, ref, sem, sem, mate).wait_send()

    def came_all(ref, sem):
        send(ref, ref, sem, sem, mate).wait_recv()

    barrier = pltpu.get_barrier_semaphore()

    def greet_ctx(i):
        pl.semaphore_signal(
            barrier, inc=1, device_id={"ctx": lax.rem(me + i, CTX)}, device_id_type=MESH
        )

    def greet_dp(i):
        pl.semaphore_signal(
            barrier, inc=1, device_id={"dp": lax.rem(zed + i, DPS)}, device_id_type=MESH
        )

    fetch = [
        pltpu.make_async_copy(src, dst, in_sem.at[i])
        for i, (src, dst) in enumerate((
            (ld_hbm, ldp.at[pl.ds(0, HEADS), :]), (raw_hbm, raw_ref), (x_hbm, xb), (cot_hbm, cot_ref),
            (w_hbm, w_ref), (b_hbm, b_ref), (skip_hbm, skip_ref),
        ))
    ]
    for copy in fetch:
        copy.start()
    loop(1, CTX, greet_ctx)
    loop(1, DPS, greet_dp)

    rows = lax.broadcasted_iota(jnp.int32, (TOK, 128), 0)
    lanes = lax.broadcasted_iota(jnp.int32, (TOK, 128), 1)
    lower = rows >= lanes
    left = lanes < WIDTH

    ldp[HEADS:, :] = jnp.zeros((128 - HEADS, TOK), F32)
    stp[...] = jnp.zeros((128, TOK), F32)
    xe[0:8, :] = jnp.zeros((8, CH), F32)
    for copy in fetch:
        copy.wait()

    sums_t = dot(ldp[...] * LOG2E, (rows <= lanes).astype(F32), precision=lax.Precision.HIGHEST)
    dst[...] = sums_t
    sums = sums_t.T
    decay = jnp.exp2(sums[TOK - 1 : TOK, :])
    dec[...] = jnp.broadcast_to(decay, (8, 128))
    for g in range(BLOCKS):
        c = slice(128 * g, 128 * g + 128)
        pair = [jnp.broadcast_to(sums[:, h : h + 1], (TOK, 128)) for h in (2 * g, 2 * g + 1)]
        dsx[:, 256 * g : 256 * g + 128] = pair[0]
        dsx[:, 256 * g + 128 : 256 * g + 256] = pair[1]
        start = jnp.exp2(jnp.where(left, pair[0], pair[1]))
        fsx[:, c] = start
        gst[:, c] = (cot_ref[:, c].astype(F32) * start).astype(BF16)

    def expand(row, count):
        at = lax.broadcasted_iota(jnp.int32, (count, 128), 1) < WIDTH
        return [
            jnp.where(
                at,
                jnp.broadcast_to(row[:, 2 * g : 2 * g + 1], (count, 128)),
                jnp.broadcast_to(row[:, 2 * g + 1 : 2 * g + 2], (count, 128)),
            )
            for g in range(BLOCKS)
        ]

    def conv(j, r0, n):
        c = cols(j)
        pre = jnp.broadcast_to(b_ref[pl.ds(j, 1), :], (n, 128))
        for k in range(TAPS):
            moved = xe[5 + k + r0 : 5 + k + r0 + n, c]
            pre = pre + w_ref[k : k + 1, c] * moved
            if k < TAPS - 1:
                xsh[k, r0 : r0 + n, c] = moved
        sig = 1.0 / (1.0 + jnp.exp(-pre))
        act[r0 : r0 + n, c] = (pre * sig).astype(BF16)
        dsil[r0 : r0 + n, c] = sig * (1.0 + pre * (1.0 - sig))

    def ends(g):
        c = cols(g)
        ds = jnp.where(left, dsx[:, cols(2 * g)], dsx[:, cols(2 * g + 1)])
        tex[:, c] = jnp.exp2(ds[TOK - 1 : TOK, :] - ds)

    def scaled(g, r0, n):
        c = cols(g)
        r = slice(r0, r0 + n)
        s = act[r, c].astype(F32)
        step = stx[r, c]
        tail[r, c] = (s * (step * tex[r, c])).astype(BF16)
        sst[r, c] = (s * step).astype(BF16)

    def later_rows(j):
        c = cols(j)
        xe[8:, c] = xb[:, c].astype(F32)
        conv(j, ROWS, TOK - ROWS)

    def later_signal(g):
        later_rows(g)
        ends(g)
        scaled(g, ROWS, TOK - ROWS)

    loop(BLOCKS, BLOCKS + 2, later_rows)

    pl.semaphore_wait(barrier, CTX - 1 + DPS - 1)

    halo_copy = send(xb.at[pl.ds(TOK - 16, 16), :], halo, h_sem.at[0], h_sem.at[1], nxt)
    halo_copy.start()
    decay_copy = send(dec, decp, d_sem.at[0], d_sem.at[1], mate)
    decay_copy.start()

    raw = raw_ref[...]
    stp[0:HEADS, :] = jnp.maximum(raw, 0.0) + jnp.log1p(jnp.exp(-jnp.abs(raw)))
    steps = stp[...].T
    for g in range(BLOCKS):
        c = slice(128 * g, 128 * g + 128)
        stx[:, c] = jnp.where(
            left,
            jnp.broadcast_to(steps[:, 2 * g : 2 * g + 1], (TOK, 128)),
            jnp.broadcast_to(steps[:, 2 * g + 1 : 2 * g + 2], (TOK, 128)),
        )
    loop(0, CUT_HALO, later_signal)

    decay_copy.wait()
    mine, other = dec[0:1, :], decp[0:1, :]
    decg[chip] = dec[...] * decp[...]

    def chip_at(i):
        return lax.rem(chip + i, CHIPS)

    def decay_out(q):
        return send(decg.at[chip], decg.at[chip], dg_s.at[0], dg_s.at[1], 2 * q + core)

    loop(1, CHIPS, lambda i: decay_out(chip_at(i)).start())
    for g, (a, b) in enumerate(zip(expand(mine, 1), expand(other, 1))):
        c = slice(128 * g, 128 * g + 128)
        coef[0:1, c] = a
        coef[1:2, c] = b

    halo_copy.wait_recv()
    xe[0:8, :] = jnp.where(me > 0, halo[...].astype(F32)[8:16, :], 0.0)
    loop(BLOCKS, BLOCKS + 2, lambda j: conv(j, 0, ROWS))
    inject = act[:, SIG : SIG + STATE]
    readout = act[:, SIG + STATE :]

    def pair_one(k, j):
        c = cols(j, GW)
        there = pl.ds(pl.multiple_of(HALF * (1 - core), HALF), HALF)
        return send(loc.at[k, there, c], prt.at[k, :, c], p1_s.at[k], p1_r.at[k, j], mate)

    readout_t = readout.T

    def local_adjoint(j):
        c = cols(j, GW)
        loc[1, :, c] = dot(readout_t, gst[:, c]).astype(BF16)
        pair_one(1, j).start()

    loop(0, GROUPS, local_adjoint)

    inject_t = inject.T

    def local_state(j):
        c = cols(j, GW)
        loc[0, :, c] = dot(inject_t, tail[:, c]).astype(BF16)
        pair_one(0, j).start()

    here = pl.ds(pl.multiple_of(HALF * core, HALF), HALF)
    own_rows = pl.ds(pl.multiple_of(ROWS * band, ROWS), ROWS)
    qc = cols(quarter, GW)

    def piece(ref, k, q):
        r = pl.ds(pl.multiple_of(ROWS * (q // 4), ROWS), ROWS)
        return ref.at[k, r, cols(lax.rem(q, 4), GW)]

    def state_out(k, q):
        return send(piece(tsum, k, q), rcv.at[k, chip], a_s.at[k], a_r.at[k], 2 * q + core)

    def chip_sums(k):
        def group(j):
            pair_one(k, j).wait_recv()
            c = cols(j, GW)
            a, b = coef[0:1, c], coef[1:2, c]
            own = loc[k, here, c].astype(F32)
            far = prt[k, :, c].astype(F32)
            if k == 0:
                total = jnp.where(first, b * own + far, a * far + own)
            else:
                total = jnp.where(first, a * far + own, b * own + far)
            tsum[k, :, c] = total.astype(BF16)

            def out(r):
                q = 4 * r + j

                @pl.when(q != chip)
                def _():
                    state_out(k, q).start()

            loop(0, 4, out)

        loop(0, GROUPS, group)
        rcv[k, chip] = tsum[k, own_rows, qc]

    def early_rows(g):
        conv(g, 0, ROWS)
        scaled(g, 0, ROWS)

    loop(CUT_HALO, CUT_PAIR, later_signal)
    chip_sums(1)
    loop(CUT_PAIR, BLOCKS, later_signal)
    loop(0, BLOCKS, early_rows, 2)
    loop(0, GROUPS, local_state)

    scores = dot(readout, inject, ((1,), (1,)))
    scores_t = dot(inject, readout, ((1,), (1,)))
    low_scores = jnp.where(lower, scores, 0.0)
    up_scores = jnp.where(rows <= lanes, scores_t, 0.0)
    run[...] = jnp.zeros((TOK, 128), F32)
    lane_a = left.astype(BF16)
    lane_b = (lanes >= WIDTH).astype(BF16)

    def intra(g):
        c = cols(g)
        fades = []
        for e in range(2):
            gap = dsx[:, cols(2 * g + e)] - dst[pl.ds(2 * g + e, 1), :]
            fades.append(jnp.exp2(jnp.where(lower, gap, -gap)))
        mix = jnp.concatenate([(f * low_scores).astype(BF16) for f in fades], axis=1)
        mix_t = jnp.concatenate([(f * up_scores).astype(BF16) for f in fades], axis=1)
        s = sst[:, c]
        t = cot_ref[:, c]
        both = jnp.concatenate([s * lane_a, s * lane_b], axis=0)
        oi[:, c] = dot(mix, both)
        bi[:, c] = dot(mix_t, jnp.concatenate([t * lane_a, t * lane_b], axis=0))
        inner = dot(t, both, ((1,), (1,)))
        run[...] += fades[0] * inner[:, :128] + fades[1] * inner[:, 128:]
        skp[:, c] = jnp.sum((act[:, c].astype(F32) * t.astype(F32)).reshape(TOK // 8, 8, 128), axis=0)

    loop(0, CUT_SUMS, intra)
    chip_sums(0)
    for g, v in enumerate(expand(skip_ref[...], 1)):
        skx[:, 128 * g : 128 * g + 128] = v
        onehot[128 * g : 128 * g + 128, :] = (
            lanes == 2 * g + (rows >= WIDTH).astype(jnp.int32)
        ).astype(BF16)
    loop(CUT_SUMS, CUT_BACK, intra)

    came_all(decg.at[pl.ds(0, CHIPS - 1)], dg_s.at[1])
    for g, v in enumerate(expand(decg[:, 0, :], CHIPS)):
        dcx[:, 128 * g : 128 * g + 128] = v

    def result_out(k, q):
        return send(res.at[k, q], piece(inc, k, chip), b_s.at[k], b_r.at[k, quarter], 2 * q + core)

    def scan(k):
        came_all(rcv.at[k, pl.ds(0, CHIPS - 1)], a_r.at[k])

        def step(i, carry):
            q = i if k == 0 else CHIPS - 1 - i
            res[k, q] = carry.astype(BF16)

            @pl.when(q != chip)
            def _():
                result_out(k, q).start()

            return dcx[pl.ds(q, 1), qc] * carry + rcv[k, q].astype(F32)

        lax.fori_loop(0, CHIPS, step, jnp.zeros((ROWS, GW), F32))
        inc[k, own_rows, qc] = res[k, chip]

    scan(1)
    loop(CUT_BACK, CUT_AHEAD, intra)
    scan(0)
    loop(CUT_AHEAD, BLOCKS, intra)

    skip_heads = sum(dot(v, onehot[...]) for v in split3(skp[...]))
    mix_total = jnp.where(lower, run[...], 0.0).astype(BF16)
    grad_readout = dot(mix_total, inject)
    grad_inject = dot(mix_total.T, readout)
    part[...] = jnp.zeros((8, CH), F32)
    part[5:6, 0:128] = jnp.sum(skip_heads, axis=0, keepdims=True)

    def pair_two(k, j):
        c = cols(j, GW)
        return send(snd.at[k, :, c], fin.at[k, here, c], p2_s.at[k], p2_r.at[k, j], mate)

    def spread(k):
        def group(j):
            c = cols(j, GW)

            @pl.when(j == quarter)
            def _():
                came_all(inc.at[k, pl.ds(0, HALF - ROWS), c], b_r.at[k, j])

            @pl.when(j != quarter)
            def _():
                came_all(inc.at[k, :, c], b_r.at[k, j])

            came = inc[k, :, c]
            wide = came.astype(F32)
            near = (coef[0:1, c] * wide + loc[k, here, c].astype(F32)).astype(BF16)
            far = (coef[1:2, c] * wide + prt[k, :, c].astype(F32)).astype(BF16)
            if k == 0:
                snd[k, :, c] = jnp.where(first, near, came)
                fin[k, here, c] = jnp.where(first, came, far)
            else:
                snd[k, :, c] = jnp.where(first, came, near)
                fin[k, here, c] = jnp.where(first, far, came)
            pair_two(k, j).start()

        loop(0, GROUPS, group)

    spread(1)

    def tile_out(j):
        return send(part.at[:, cols(j)], ar1.at[me], r1_s.at[0], r1_s.at[1], j)

    def each_other(i, fn):
        @pl.when(i != me)
        def _():
            fn(i)

    def finish_rows(j, grad_act):
        c = cols(j)
        grad = grad_act * dsil[:, c]
        gp[0:TOK, c] = grad
        for k in range(TAPS):
            moved = xe[8:, c] if k == TAPS - 1 else xsh[k, :, c]
            part[k : k + 1, c] = jnp.sum(grad * moved, axis=0, keepdims=True)
        part[4:5, c] = jnp.sum(grad, axis=0, keepdims=True)
        each_other(j, lambda j: tile_out(j).start())

    def finish(g, i):
        c = cols(g)
        s = act[:, c].astype(F32)
        t = cot_ref[:, c].astype(F32)
        back = bi[:, c] + tex[:, c] * tmp[:, cols(i)]
        z = s * back
        z_hi = z.astype(BF16)
        zhi[:, c] = z_hi
        zlo[:, c] = (z - z_hi.astype(F32)).astype(BF16)
        finish_rows(g, stx[:, c] * back + skx[:, c] * t)

    def finish_group(j):
        pair_two(1, j).wait_recv()
        tmp[...] = dot(inject, fin[1, :, cols(j, GW)])
        loop(0, GB, lambda i: finish(j * GB + i, i))

    loop(0, GROUPS, finish_group)
    finish_rows(BLOCKS, grad_inject + dot(tail[...], fin[1], ((1,), (1,))))
    spread(0)
    loop(0, GROUPS, lambda j: pair_two(0, j).wait_recv())
    finish_rows(BLOCKS + 1, grad_readout + dot(gst[...], fin[0], ((1,), (1,))))

    grad_halo = send(gp.at[pl.ds(0, 8), :], gp.at[pl.ds(TOK, 8), :], g_sem.at[0], g_sem.at[1], prv)
    grad_halo.start()

    def output(g, i):
        c = cols(g)
        out = oi[:, c] + fsx[:, c] * tmp[:, cols(i)] + skx[:, c] * act[:, c].astype(F32)
        out_ref[:, c] = out.astype(BF16)

    def output_group(j):
        tmp[...] = dot(readout, fin[0, :, cols(j, GW)])
        loop(0, GB, lambda i: output(j * GB + i, i))

    loop(0, GROUPS, output_group)
    out_copy = pltpu.make_async_copy(out_ref, out_hbm, o_sem.at[0])
    out_copy.start()

    def dp_out(i):
        z = lax.rem(zed + i, DPS)
        return pltpu.make_async_remote_copy(
            src_ref=sum1, dst_ref=ar2.at[zed], send_sem=r2_s.at[0], recv_sem=r2_s.at[1],
            device_id={"dp": z}, device_id_type=MESH,
        )

    def total_out(i):
        return send(tot.at[:, cols(me)], tot.at[:, cols(me)], r3_s.at[0], r3_s.at[1], i)

    owner = me < OWNERS

    @pl.when(owner)
    def _():
        came_all(ar1.at[pl.ds(0, CTX - 1)], r1_s.at[1])
        ar1[me] = part[:, cols(me)]
        sum1[...] = jnp.sum(ar1[...], axis=0)
        loop(1, DPS, lambda i: dp_out(i).start())

    steps_z = dot(zhi[...], onehot[...]) + dot(zlo[...], onehot[...])
    e = jnp.exp(-jnp.abs(raw))
    gate = jnp.where(raw >= 0, 1.0, e) / (1.0 + e)
    sg_ref[...] = steps_z.T[0:HEADS, :] * gate

    grad_halo.wait_recv()
    gp[TOK:, :] = jnp.where(me < CTX - 1, gp[TOK:, :], 0.0)

    def input_grad(j):
        c = cols(j)
        total = w_ref[0:1, c] * gp[3 : 3 + TOK, c]
        for k in range(1, TAPS):
            total = total + w_ref[k : k + 1, c] * gp[3 - k : 3 - k + TOK, c]
        gin_ref[:, c] = total.astype(BF16)

    loop(0, CH // 256, input_grad)

    @pl.when(owner)
    def _():
        came_all(ar2.at[pl.ds(0, DPS - 1)], r2_s.at[1])
        ar2[zed] = sum1[...]
        tot[:, cols(me)] = jnp.sum(ar2[...], axis=0)
        loop(0, CTX, lambda i: each_other(i, lambda i: total_out(i).start()))

    loop(CH // 256, CH // 128, input_grad)
    gin_copy = pltpu.make_async_copy(gin_ref, gin_hbm, o_sem.at[1])
    gin_copy.start()

    halo_copy.wait_send()
    grad_halo.wait_send()

    left_all(decg.at[pl.ds(0, CHIPS - 1)], dg_s.at[0])
    for k in range(2):
        left_all(tsum.at[k], p1_s.at[k])
        left_all(tsum.at[k], p2_s.at[k])
        left_all(rcv.at[k, pl.ds(0, CHIPS - 1)], a_s.at[k])
        left_all(rcv.at[k, pl.ds(0, CHIPS - 1)], b_s.at[k])

    @pl.when(owner)
    def _():
        some = tot.at[:, pl.ds(0, CH - 128)]
        left_all(some, r1_s.at[0])
        left_all(ar2.at[pl.ds(0, DPS - 1)], r2_s.at[0])
        left_all(ar1.at[pl.ds(0, CTX - 1)], r3_s.at[0])
        came_all(some, r3_s.at[1])

    @pl.when(jnp.logical_not(owner))
    def _():
        left_all(tot, r1_s.at[0])
        came_all(tot, r3_s.at[1])

    wg_ref[...] = tot[0:TAPS, :]
    for j in range(OWNERS):
        bg_ref[j : j + 1, :] = tot[4:5, 128 * j : 128 * j + 128]
    kg_ref[...] = tot[5:6, 0:HEADS]
    out_copy.wait()
    gin_copy.wait()


def copy_kernel(*refs):
    n = (len(refs) - 2) // 3
    src, dst, via, (isem, osem) = refs[:n], refs[n : 2 * n], refs[2 * n : 3 * n], refs[3 * n :]
    first = [pltpu.make_async_copy(src[i], via[i], isem.at[i]) for i in range(n)]
    second = [pltpu.make_async_copy(via[i], dst[i], osem.at[i]) for i in range(n)]
    for copy in first:
        copy.start()
    for a, b in zip(first, second):
        a.wait()
        b.start()
    for copy in second:
        copy.wait()


def scratch():
    v = pltpu.VMEM
    dma = pltpu.SemaphoreType.DMA
    return [
        v((TOK, SIG), BF16),
        v((TOK, CH), BF16),
        v((TOK, CH), BF16),
        v((TOK, SIG), BF16),
        v((TAPS, CH), F32),
        v((OWNERS, 128), F32),
        v((1, HEADS), F32),
        v((HEADS, TOK), F32),
        v((TOK + 8, CH), F32),
        v((16, CH), BF16),
        v((TOK, CH), BF16),
        v((TOK, CH), F32),
        v((128, TOK), F32),
        v((128, TOK), F32),
        v((128, TOK), F32),
        v((TOK, HEADS * 128), F32),
        v((TOK, SIG), F32),
        v((TOK, SIG), F32),
        v((TOK, SIG), F32),
        v((TOK, SIG), BF16),
        v((TOK, SIG), BF16),
        v((TOK, SIG), BF16),
        v((2, STATE, SIG), BF16),
        v((2, HALF, SIG), BF16),
        v((8, 128), F32),
        v((8, 128), F32),
        v((CHIPS, 8, 128), F32),
        v((CHIPS, SIG), F32),
        v((8, SIG), F32),
        v((1, SIG), F32),
        v((2, HALF, SIG), BF16),
        v((2, CHIPS, ROWS, GW), BF16),
        v((2, CHIPS, ROWS, GW), BF16),
        v((2, HALF, SIG), BF16),
        v((2, HALF, SIG), BF16),
        v((2, STATE, SIG), BF16),
        v((TOK, SIG), F32),
        v((TOK, SIG), F32),
        v((TOK, 128), F32),
        v((TOK, GW), F32),
        v((TAPS - 1, TOK, CH), F32),
        v((TOK + 8, CH), F32),
        v((TOK, SIG), BF16),
        v((TOK, SIG), BF16),
        v((SIG, 128), BF16),
        v((8, SIG), F32),
        v((8, CH), F32),
        v((CTX, 8, 128), F32),
        v((DPS, 8, 128), F32),
        v((8, 128), F32),
        v((8, CH), F32),
        dma((7,)),
        dma((2,)),
        dma((2,)),
        dma((2,)),
        dma((2,)),
        dma((2,)),
        dma((2, GROUPS)),
        dma((2,)),
        dma((2,)),
        dma((2,)),
        dma((2, GROUPS)),
        dma((2,)),
        dma((2, GROUPS)),
        dma((2,)),
        dma((2,)),
        dma((2,)),
        dma((2,)),
    ]


def body(conv_input, step_raw, log_decay, cotangent, conv_weight, conv_bias, skip_gain):
    vmem = pl.BlockSpec(memory_space=pltpu.VMEM)
    hbm = pl.BlockSpec(memory_space=pltpu.HBM)
    shapes = (
        jax.ShapeDtypeStruct((TOK, SIG), BF16),
        jax.ShapeDtypeStruct((TOK, CH), BF16),
        jax.ShapeDtypeStruct((HEADS, TOK), F32),
        jax.ShapeDtypeStruct((TAPS, CH), F32),
        jax.ShapeDtypeStruct((OWNERS, 128), F32),
        jax.ShapeDtypeStruct((1, HEADS), F32),
    )
    results = pl.pallas_call(
        kernel,
        out_shape=shapes,
        in_specs=[hbm] * 7,
        out_specs=[hbm] * 2 + [vmem] * 4,
        scratch_shapes=scratch(),
        compiler_params=pltpu.CompilerParams(
            collective_id=0, has_side_effects=True, vmem_limit_bytes=VMEM
        ),
    )(
        conv_input[0], step_raw[0].T, log_decay[0].T, cotangent[0],
        conv_weight, conv_bias.reshape(OWNERS, 128), skip_gain[None],
    )
    out, gin, sg, wg, bg, kg = pl.pallas_call(
        copy_kernel,
        out_shape=shapes,
        in_specs=[hbm] * 6,
        out_specs=[hbm] * 6,
        scratch_shapes=[pltpu.VMEM(a.shape, a.dtype) for a in shapes]
        + [pltpu.SemaphoreType.DMA((6,))] * 2,
        compiler_params=pltpu.CompilerParams(vmem_limit_bytes=VMEM),
    )(*results)
    return out[None], gin[None], sg.T[None], wg, bg.reshape(CH), kg[0]


def solution(mesh):
    split = P("dp", "ctx", None)
    return jax.shard_map(
        body,
        mesh=mesh,
        in_specs=(split, split, split, split, P(), P(), P()),
        out_specs=(split, split, split, P(), P(), P()),
        check_vma=False,
    )
```

```python
import jax
import jax.numpy as jnp
from jax import lax
from jax.experimental import pallas as pl
from jax.experimental.pallas import tpu as pltpu
from jax.sharding import PartitionSpec as P

HEADS = 40
WIDTH = 64
STATE = 128
TAPS = 4
TOK = 128
SIG = HEADS * WIDTH
CH = SIG + 2 * STATE
BLOCKS = SIG // 128
CTX = 32
CHIPS = 16
DPS = 8
GROUPS = 4
GW = SIG // GROUPS
GB = GW // 128
HALF = STATE // 2
ROWS = 16
OWNERS = CH // 128
CUT_HALO = 6
CUT_PAIR = 12
CUT_SUMS = 3
CUT_BACK = 8
CUT_AHEAD = 14
VMEM = 48 * 1024 * 1024
LOG2E = 1.4426950408889634
F32 = jnp.float32
BF16 = jnp.bfloat16
MESH = pl.DeviceIdType.MESH


def dot(a, b, dims=((1,), (0,)), **kw):
    return lax.dot_general(a, b, (dims, ((), ())), preferred_element_type=F32, **kw)


def split3(v):
    hi = v.astype(BF16)
    rest = v - hi.astype(F32)
    mid = rest.astype(BF16)
    low = (rest - mid.astype(F32)).astype(BF16)
    return hi, mid, low


def loop(lo, hi, fn, unroll=1):
    whole = lo + (hi - lo) // unroll * unroll

    def step(i, carry):
        for k in range(unroll):
            fn(lo + i * unroll + k)
        return carry

    if whole > lo:
        lax.fori_loop(0, (whole - lo) // unroll, step, 0)
    for i in range(whole, hi):
        fn(jnp.int32(i))


def cols(i, width=128):
    return pl.ds(pl.multiple_of(i * width, 128), width)


def kernel(
    x_hbm, raw_hbm, ld_hbm, cot_hbm, w_hbm, b_hbm, skip_hbm,
    out_ref, gin_ref, sg_ref, wg_ref, bg_ref, kg_ref,
    xb, cot_ref, w_ref, b_ref, skip_ref, raw_ref,
    xe, halo, act, dsil, ldp, stp, dst, dsx, stx, fsx, tex, tail, gst, sst,
    loc, prt, dec, decp, decg, dcx, coef, skx, tsum, rcv, res, inc, snd, fin,
    oi, bi, run, tmp, xsh, gp, zhi, zlo, onehot, skp, part, ar1, ar2, sum1, tot,
    in_sem, h_sem, d_sem, dg_s, p1_s, p1_r, a_s, a_r, b_s, b_r, p2_s, p2_r, g_sem,
    r1_s, r2_s, r3_s,
):
    me = lax.axis_index("ctx")
    zed = lax.axis_index("dp")
    core = lax.rem(me, 2)
    chip = me // 2
    quarter = lax.rem(chip, 4)
    band = chip // 4
    mate = me + 1 - 2 * core
    nxt = lax.rem(me + 1, CTX)
    prv = lax.rem(me + CTX - 1, CTX)
    first = core == 0

    def send(src, dst, ssem, rsem, ctx):
        return pltpu.make_async_remote_copy(
            src_ref=src, dst_ref=dst, send_sem=ssem, recv_sem=rsem,
            device_id={"ctx": ctx}, device_id_type=MESH,
        )

    def turned(i, own):
        away = jnp.where(i == 0, 2, jnp.where(i == 1, 1, jnp.where(i == 2, 3, 0)))
        return lax.rem(own + away, 4)

    def left_all(ref, sem):
        send(ref, ref, sem, sem, mate).wait_send()

    def came_all(ref, sem):
        send(ref, ref, sem, sem, mate).wait_recv()

    barrier = pltpu.get_barrier_semaphore()

    def greet_ctx(i):
        pl.semaphore_signal(
            barrier, inc=1, device_id={"ctx": lax.rem(me + i, CTX)}, device_id_type=MESH
        )

    def greet_dp(i):
        pl.semaphore_signal(
            barrier, inc=1, device_id={"dp": lax.rem(zed + i, DPS)}, device_id_type=MESH
        )

    fetch = [
        pltpu.make_async_copy(src, dst, in_sem.at[i])
        for i, (src, dst) in enumerate((
            (ld_hbm, ldp.at[pl.ds(0, HEADS), :]), (raw_hbm, raw_ref), (x_hbm, xb), (cot_hbm, cot_ref),
            (w_hbm, w_ref), (b_hbm, b_ref), (skip_hbm, skip_ref),
        ))
    ]
    for copy in fetch:
        copy.start()
    loop(1, CTX, greet_ctx)
    loop(1, DPS, greet_dp)

    rows = lax.broadcasted_iota(jnp.int32, (TOK, 128), 0)
    lanes = lax.broadcasted_iota(jnp.int32, (TOK, 128), 1)
    lower = rows >= lanes
    left = lanes < WIDTH

    ldp[HEADS:, :] = jnp.zeros((128 - HEADS, TOK), F32)
    stp[...] = jnp.zeros((128, TOK), F32)
    xe[0:8, :] = jnp.zeros((8, CH), F32)
    for copy in fetch:
        copy.wait()

    sums_t = dot(ldp[...] * LOG2E, (rows <= lanes).astype(F32), precision=lax.Precision.HIGHEST)
    dst[...] = sums_t
    sums = sums_t.T
    decay = jnp.exp2(sums[TOK - 1 : TOK, :])
    dec[...] = jnp.broadcast_to(decay, (8, 128))
    for g in range(BLOCKS):
        c = slice(128 * g, 128 * g + 128)
        pair = [jnp.broadcast_to(sums[:, h : h + 1], (TOK, 128)) for h in (2 * g, 2 * g + 1)]
        dsx[:, 256 * g : 256 * g + 128] = pair[0]
        dsx[:, 256 * g + 128 : 256 * g + 256] = pair[1]
        start = jnp.exp2(jnp.where(left, pair[0], pair[1]))
        fsx[:, c] = start
        gst[:, c] = (cot_ref[:, c].astype(F32) * start).astype(BF16)

    def expand(row, count):
        at = lax.broadcasted_iota(jnp.int32, (count, 128), 1) < WIDTH
        return [
            jnp.where(
                at,
                jnp.broadcast_to(row[:, 2 * g : 2 * g + 1], (count, 128)),
                jnp.broadcast_to(row[:, 2 * g + 1 : 2 * g + 2], (count, 128)),
            )
            for g in range(BLOCKS)
        ]

    def conv(j, r0, n):
        c = cols(j)
        pre = jnp.broadcast_to(b_ref[pl.ds(j, 1), :], (n, 128))
        for k in range(TAPS):
            moved = xe[5 + k + r0 : 5 + k + r0 + n, c]
            pre = pre + w_ref[k : k + 1, c] * moved
            if k < TAPS - 1:
                xsh[k, r0 : r0 + n, c] = moved
        sig = 1.0 / (1.0 + jnp.exp(-pre))
        act[r0 : r0 + n, c] = (pre * sig).astype(BF16)
        dsil[r0 : r0 + n, c] = sig * (1.0 + pre * (1.0 - sig))

    def ends(g):
        c = cols(g)
        ds = jnp.where(left, dsx[:, cols(2 * g)], dsx[:, cols(2 * g + 1)])
        tex[:, c] = jnp.exp2(ds[TOK - 1 : TOK, :] - ds)

    def scaled(g, r0, n):
        c = cols(g)
        r = slice(r0, r0 + n)
        s = act[r, c].astype(F32)
        step = stx[r, c]
        tail[r, c] = (s * (step * tex[r, c])).astype(BF16)
        sst[r, c] = (s * step).astype(BF16)

    def later_rows(j):
        c = cols(j)
        xe[8:, c] = xb[:, c].astype(F32)
        conv(j, ROWS, TOK - ROWS)

    def later_signal(g):
        later_rows(g)
        ends(g)
        scaled(g, ROWS, TOK - ROWS)

    loop(BLOCKS, BLOCKS + 2, later_rows)

    pl.semaphore_wait(barrier, CTX - 1 + DPS - 1)

    halo_copy = send(xb.at[pl.ds(TOK - 16, 16), :], halo, h_sem.at[0], h_sem.at[1], nxt)
    halo_copy.start()
    decay_copy = send(dec, decp, d_sem.at[0], d_sem.at[1], mate)
    decay_copy.start()

    raw = raw_ref[...]
    stp[0:HEADS, :] = jnp.maximum(raw, 0.0) + jnp.log1p(jnp.exp(-jnp.abs(raw)))
    steps = stp[...].T
    for g in range(BLOCKS):
        c = slice(128 * g, 128 * g + 128)
        stx[:, c] = jnp.where(
            left,
            jnp.broadcast_to(steps[:, 2 * g : 2 * g + 1], (TOK, 128)),
            jnp.broadcast_to(steps[:, 2 * g + 1 : 2 * g + 2], (TOK, 128)),
        )
    loop(0, CUT_HALO, later_signal, 2)

    decay_copy.wait()
    mine, other = dec[0:1, :], decp[0:1, :]
    decg[chip] = dec[...] * decp[...]

    def chip_at(i):
        return lax.rem(chip + i, CHIPS)

    def decay_out(q):
        return send(decg.at[chip], decg.at[chip], dg_s.at[0], dg_s.at[1], 2 * q + core)

    loop(1, CHIPS, lambda i: decay_out(chip_at(i)).start())
    for g, (a, b) in enumerate(zip(expand(mine, 1), expand(other, 1))):
        c = slice(128 * g, 128 * g + 128)
        coef[0:1, c] = a
        coef[1:2, c] = b

    halo_copy.wait_recv()
    xe[0:8, :] = jnp.where(me > 0, halo[...].astype(F32)[8:16, :], 0.0)
    loop(BLOCKS, BLOCKS + 2, lambda j: conv(j, 0, ROWS))
    inject = act[:, SIG : SIG + STATE]
    readout = act[:, SIG + STATE :]

    def pair_one(k, j):
        c = cols(j, GW)
        there = pl.ds(pl.multiple_of(HALF * (1 - core), HALF), HALF)
        return send(loc.at[k, there, c], prt.at[k, :, c], p1_s.at[k], p1_r.at[k, j], mate)

    readout_t = readout.T

    def local_adjoint(i):
        j = turned(i, quarter)
        c = cols(j, GW)
        loc[1, :, c] = dot(readout_t, gst[:, c]).astype(BF16)
        pair_one(1, j).start()

    loop(0, GROUPS, local_adjoint)

    inject_t = inject.T

    def local_state(i):
        j = turned(i, quarter)
        c = cols(j, GW)
        loc[0, :, c] = dot(inject_t, tail[:, c]).astype(BF16)
        pair_one(0, j).start()

    here = pl.ds(pl.multiple_of(HALF * core, HALF), HALF)
    own_rows = pl.ds(pl.multiple_of(ROWS * band, ROWS), ROWS)
    qc = cols(quarter, GW)

    def piece(ref, k, q):
        r = pl.ds(pl.multiple_of(ROWS * (q // 4), ROWS), ROWS)
        return ref.at[k, r, cols(lax.rem(q, 4), GW)]

    def state_out(k, q):
        return send(piece(tsum, k, q), rcv.at[k, chip], a_s.at[k], a_r.at[k], 2 * q + core)

    def chip_sums(k):
        def group(i):
            j = turned(i, quarter)
            pair_one(k, j).wait_recv()
            c = cols(j, GW)
            a, b = coef[0:1, c], coef[1:2, c]
            own = loc[k, here, c].astype(F32)
            far = prt[k, :, c].astype(F32)
            if k == 0:
                total = jnp.where(first, b * own + far, a * far + own)
            else:
                total = jnp.where(first, a * far + own, b * own + far)
            tsum[k, :, c] = total.astype(BF16)

            def out(r):
                q = 4 * turned(r, band) + j

                @pl.when(q != chip)
                def _():
                    state_out(k, q).start()

            loop(0, 4, out)

        loop(0, GROUPS, group)
        rcv[k, chip] = tsum[k, own_rows, qc]

    def early_rows(g):
        conv(g, 0, ROWS)
        scaled(g, 0, ROWS)

    loop(CUT_HALO, CUT_PAIR, later_signal, 2)
    chip_sums(1)
    loop(CUT_PAIR, BLOCKS, later_signal, 2)
    loop(0, BLOCKS, early_rows, 2)
    loop(0, GROUPS, local_state)

    scores = dot(readout, inject, ((1,), (1,)))
    scores_t = dot(inject, readout, ((1,), (1,)))
    low_scores = jnp.where(lower, scores, 0.0)
    up_scores = jnp.where(rows <= lanes, scores_t, 0.0)
    run[...] = jnp.zeros((TOK, 128), F32)
    lane_a = left.astype(BF16)
    lane_b = (lanes >= WIDTH).astype(BF16)

    def intra(g):
        c = cols(g)
        fades = []
        for e in range(2):
            gap = dsx[:, cols(2 * g + e)] - dst[pl.ds(2 * g + e, 1), :]
            fades.append(jnp.exp2(jnp.where(lower, gap, -gap)))
        mix = jnp.concatenate([(f * low_scores).astype(BF16) for f in fades], axis=1)
        mix_t = jnp.concatenate([(f * up_scores).astype(BF16) for f in fades], axis=1)
        s = sst[:, c]
        t = cot_ref[:, c]
        both = jnp.concatenate([s * lane_a, s * lane_b], axis=0)
        oi[:, c] = dot(mix, both)
        bi[:, c] = dot(mix_t, jnp.concatenate([t * lane_a, t * lane_b], axis=0))
        inner = dot(t, both, ((1,), (1,)))
        run[...] += fades[0] * inner[:, :128] + fades[1] * inner[:, 128:]
        skp[:, c] = jnp.sum((act[:, c].astype(F32) * t.astype(F32)).reshape(TOK // 8, 8, 128), axis=0)

    loop(0, CUT_SUMS, intra, 2)
    chip_sums(0)
    for g, v in enumerate(expand(skip_ref[...], 1)):
        skx[:, 128 * g : 128 * g + 128] = v
        onehot[128 * g : 128 * g + 128, :] = (
            lanes == 2 * g + (rows >= WIDTH).astype(jnp.int32)
        ).astype(BF16)
    loop(CUT_SUMS, CUT_BACK, intra, 2)

    came_all(decg.at[pl.ds(0, CHIPS - 1)], dg_s.at[1])
    for g, v in enumerate(expand(decg[:, 0, :], CHIPS)):
        dcx[:, 128 * g : 128 * g + 128] = v

    def result_out(k, q):
        return send(res.at[k, q], piece(inc, k, chip), b_s.at[k], b_r.at[k, quarter], 2 * q + core)

    def scan(k):
        came_all(rcv.at[k, pl.ds(0, CHIPS - 1)], a_r.at[k])

        def step(i, carry):
            q = i if k == 0 else CHIPS - 1 - i
            res[k, q] = carry.astype(BF16)
            return dcx[pl.ds(q, 1), qc] * carry + rcv[k, q].astype(F32)

        lax.fori_loop(0, CHIPS, step, jnp.zeros((ROWS, GW), F32))

        def out(i):
            q = 4 * turned(i // 4, band) + turned(lax.rem(i, 4), quarter)
            result_out(k, q).start()

        loop(0, CHIPS - 1, out)
        inc[k, own_rows, qc] = res[k, chip]

    scan(1)
    loop(CUT_BACK, CUT_AHEAD, intra, 2)
    scan(0)
    loop(CUT_AHEAD, BLOCKS, intra, 2)

    skip_heads = sum(dot(v, onehot[...]) for v in split3(skp[...]))
    mix_total = jnp.where(lower, run[...], 0.0).astype(BF16)
    grad_readout = dot(mix_total, inject)
    grad_inject = dot(mix_total.T, readout)
    part[...] = jnp.zeros((8, CH), F32)
    part[5:6, 0:128] = jnp.sum(skip_heads, axis=0, keepdims=True)

    def pair_two(k, j):
        c = cols(j, GW)
        return send(snd.at[k, :, c], fin.at[k, here, c], p2_s.at[k], p2_r.at[k, j], mate)

    def spread(k):
        def group(i):
            j = lax.rem(quarter + i, 4)
            c = cols(j, GW)

            @pl.when(j == quarter)
            def _():
                came_all(inc.at[k, pl.ds(0, HALF - ROWS), c], b_r.at[k, j])

            @pl.when(j != quarter)
            def _():
                came_all(inc.at[k, :, c], b_r.at[k, j])

            came = inc[k, :, c]
            wide = came.astype(F32)
            near = (coef[0:1, c] * wide + loc[k, here, c].astype(F32)).astype(BF16)
            far = (coef[1:2, c] * wide + prt[k, :, c].astype(F32)).astype(BF16)
            if k == 0:
                snd[k, :, c] = jnp.where(first, near, came)
                fin[k, here, c] = jnp.where(first, came, far)
            else:
                snd[k, :, c] = jnp.where(first, came, near)
                fin[k, here, c] = jnp.where(first, far, came)
            pair_two(k, j).start()

        loop(0, GROUPS, group)

    spread(1)

    def tile_out(j):
        return send(part.at[:, cols(j)], ar1.at[me], r1_s.at[0], r1_s.at[1], j)

    def each_other(i, fn):
        @pl.when(i != me)
        def _():
            fn(i)

    def finish_rows(j, grad_act):
        c = cols(j)
        grad = grad_act * dsil[:, c]
        gp[0:TOK, c] = grad
        for k in range(TAPS):
            moved = xe[8:, c] if k == TAPS - 1 else xsh[k, :, c]
            part[k : k + 1, c] = jnp.sum(grad * moved, axis=0, keepdims=True)
        part[4:5, c] = jnp.sum(grad, axis=0, keepdims=True)

    def finish(g, i):
        c = cols(g)
        s = act[:, c].astype(F32)
        t = cot_ref[:, c].astype(F32)
        back = bi[:, c] + tex[:, c] * tmp[:, cols(i)]
        z = s * back
        z_hi = z.astype(BF16)
        zhi[:, c] = z_hi
        zlo[:, c] = (z - z_hi.astype(F32)).astype(BF16)
        finish_rows(g, stx[:, c] * back + skx[:, c] * t)

    def finish_group(i):
        j = lax.rem(quarter + i, 4)
        pair_two(1, j).wait_recv()
        tmp[...] = dot(inject, fin[1, :, cols(j, GW)])
        loop(0, GB, lambda i: finish(j * GB + i, i), GB)
        loop(0, GB, lambda i: each_other(j * GB + i, lambda t: tile_out(t).start()))

    loop(0, GROUPS, finish_group)
    finish_rows(BLOCKS, grad_inject + dot(tail[...], fin[1], ((1,), (1,))))
    each_other(BLOCKS, lambda j: tile_out(j).start())
    spread(0)
    loop(0, GROUPS, lambda j: pair_two(0, j).wait_recv())
    finish_rows(BLOCKS + 1, grad_readout + dot(gst[...], fin[0], ((1,), (1,))))
    each_other(OWNERS - 1, lambda j: tile_out(j).start())

    grad_halo = send(gp.at[pl.ds(0, 8), :], gp.at[pl.ds(TOK, 8), :], g_sem.at[0], g_sem.at[1], prv)
    grad_halo.start()

    def output(g, i):
        c = cols(g)
        out = oi[:, c] + fsx[:, c] * tmp[:, cols(i)] + skx[:, c] * act[:, c].astype(F32)
        out_ref[:, c] = out.astype(BF16)

    def output_group(j):
        tmp[...] = dot(readout, fin[0, :, cols(j, GW)])
        loop(0, GB, lambda i: output(j * GB + i, i))

    loop(0, GROUPS, output_group)

    def dp_out(i):
        z = lax.rem(zed + i, DPS)
        return pltpu.make_async_remote_copy(
            src_ref=sum1, dst_ref=ar2.at[zed], send_sem=r2_s.at[0], recv_sem=r2_s.at[1],
            device_id={"dp": z}, device_id_type=MESH,
        )

    def total_out(i):
        return send(tot.at[:, cols(me)], tot.at[:, cols(me)], r3_s.at[0], r3_s.at[1], i)

    owner = me < OWNERS

    @pl.when(owner)
    def _():
        came_all(ar1.at[pl.ds(0, CTX - 1)], r1_s.at[1])
        ar1[me] = part[:, cols(me)]
        sum1[...] = jnp.sum(ar1[...], axis=0)
        loop(1, DPS, lambda i: dp_out(i).start())

    steps_z = dot(zhi[...], onehot[...]) + dot(zlo[...], onehot[...])
    e = jnp.exp(-jnp.abs(raw))
    gate = jnp.where(raw >= 0, 1.0, e) / (1.0 + e)
    sg_ref[...] = steps_z.T[0:HEADS, :] * gate

    grad_halo.wait_recv()
    gp[TOK:, :] = jnp.where(me < CTX - 1, gp[TOK:, :], 0.0)

    def input_grad(j):
        c = cols(j)
        total = w_ref[0:1, c] * gp[3 : 3 + TOK, c]
        for k in range(1, TAPS):
            total = total + w_ref[k : k + 1, c] * gp[3 - k : 3 - k + TOK, c]
        gin_ref[:, c] = total.astype(BF16)

    loop(0, CH // 256, input_grad)

    @pl.when(owner)
    def _():
        came_all(ar2.at[pl.ds(0, DPS - 1)], r2_s.at[1])
        ar2[zed] = sum1[...]
        tot[:, cols(me)] = jnp.sum(ar2[...], axis=0)
        loop(1, CTX, lambda i: total_out(lax.rem(me + i, CTX)).start())

    loop(CH // 256, CH // 128, input_grad)

    halo_copy.wait_send()
    grad_halo.wait_send()

    left_all(decg.at[pl.ds(0, CHIPS - 1)], dg_s.at[0])
    for k in range(2):
        left_all(tsum.at[k], p1_s.at[k])
        left_all(tsum.at[k], p2_s.at[k])
        left_all(rcv.at[k, pl.ds(0, CHIPS - 1)], a_s.at[k])
        left_all(rcv.at[k, pl.ds(0, CHIPS - 1)], b_s.at[k])

    @pl.when(owner)
    def _():
        some = tot.at[:, pl.ds(0, CH - 128)]
        left_all(some, r1_s.at[0])
        left_all(ar2.at[pl.ds(0, DPS - 1)], r2_s.at[0])
        left_all(ar1.at[pl.ds(0, CTX - 1)], r3_s.at[0])
        came_all(some, r3_s.at[1])

    @pl.when(jnp.logical_not(owner))
    def _():
        left_all(tot, r1_s.at[0])
        came_all(tot, r3_s.at[1])

    wg_ref[...] = tot[0:TAPS, :]
    for j in range(OWNERS):
        bg_ref[j : j + 1, :] = tot[4:5, 128 * j : 128 * j + 128]
    kg_ref[...] = tot[5:6, 0:HEADS]


def copy_kernel(*refs):
    n = len(refs) // 2
    copies = [pltpu.make_async_copy(refs[i], refs[n + i], refs[-1].at[i]) for i in range(n)]
    for copy in copies:
        copy.start()
    for copy in copies:
        copy.wait()


def scratch():
    v = pltpu.VMEM
    dma = pltpu.SemaphoreType.DMA
    return [
        v((TOK, CH), BF16),
        v((TOK, SIG), BF16),
        v((TAPS, CH), F32),
        v((OWNERS, 128), F32),
        v((1, HEADS), F32),
        v((HEADS, TOK), F32),
        v((TOK + 8, CH), F32),
        v((16, CH), BF16),
        v((TOK, CH), BF16),
        v((TOK, CH), F32),
        v((128, TOK), F32),
        v((128, TOK), F32),
        v((128, TOK), F32),
        v((TOK, HEADS * 128), F32),
        v((TOK, SIG), F32),
        v((TOK, SIG), F32),
        v((TOK, SIG), F32),
        v((TOK, SIG), BF16),
        v((TOK, SIG), BF16),
        v((TOK, SIG), BF16),
        v((2, STATE, SIG), BF16),
        v((2, HALF, SIG), BF16),
        v((8, 128), F32),
        v((8, 128), F32),
        v((CHIPS, 8, 128), F32),
        v((CHIPS, SIG), F32),
        v((8, SIG), F32),
        v((1, SIG), F32),
        v((2, HALF, SIG), BF16),
        v((2, CHIPS, ROWS, GW), BF16),
        v((2, CHIPS, ROWS, GW), BF16),
        v((2, HALF, SIG), BF16),
        v((2, HALF, SIG), BF16),
        v((2, STATE, SIG), BF16),
        v((TOK, SIG), F32),
        v((TOK, SIG), F32),
        v((TOK, 128), F32),
        v((TOK, GW), F32),
        v((TAPS - 1, TOK, CH), F32),
        v((TOK + 8, CH), F32),
        v((TOK, SIG), BF16),
        v((TOK, SIG), BF16),
        v((SIG, 128), BF16),
        v((8, SIG), F32),
        v((8, CH), F32),
        v((CTX, 8, 128), F32),
        v((DPS, 8, 128), F32),
        v((8, 128), F32),
        v((8, CH), F32),
        dma((7,)),
        dma((2,)),
        dma((2,)),
        dma((2,)),
        dma((2,)),
        dma((2, GROUPS)),
        dma((2,)),
        dma((2,)),
        dma((2,)),
        dma((2, GROUPS)),
        dma((2,)),
        dma((2, GROUPS)),
        dma((2,)),
        dma((2,)),
        dma((2,)),
        dma((2,)),
    ]


def body(conv_input, step_raw, log_decay, cotangent, conv_weight, conv_bias, skip_gain):
    vmem = pl.BlockSpec(memory_space=pltpu.VMEM)
    hbm = pl.BlockSpec(memory_space=pltpu.HBM)
    shapes = (
        jax.ShapeDtypeStruct((TOK, SIG), BF16),
        jax.ShapeDtypeStruct((TOK, CH), BF16),
        jax.ShapeDtypeStruct((HEADS, TOK), F32),
        jax.ShapeDtypeStruct((TAPS, CH), F32),
        jax.ShapeDtypeStruct((OWNERS, 128), F32),
        jax.ShapeDtypeStruct((1, HEADS), F32),
    )
    results = pl.pallas_call(
        kernel,
        out_shape=[pltpu.VMEM(a.shape, a.dtype) for a in shapes],
        in_specs=[hbm] * 7,
        out_specs=[vmem] * 6,
        scratch_shapes=scratch(),
        compiler_params=pltpu.CompilerParams(
            collective_id=0, has_side_effects=True, vmem_limit_bytes=VMEM
        ),
    )(*(pltpu.with_memory_space_constraint(a, pltpu.HBM) for a in (
        conv_input[0], step_raw[0].T, log_decay[0].T, cotangent[0],
        conv_weight, conv_bias.reshape(OWNERS, 128), skip_gain[None],
    )))
    out, gin, sg, wg, bg, kg = pl.pallas_call(
        copy_kernel,
        out_shape=shapes,
        in_specs=[vmem] * 6,
        out_specs=[hbm] * 6,
        scratch_shapes=[pltpu.SemaphoreType.DMA((6,))],
    )(*(pltpu.with_memory_space_constraint(a, pltpu.VMEM) for a in results))
    return out[None], gin[None], sg.T[None], wg, bg.reshape(CH), kg[0]


def solution(mesh):
    split = P("dp", "ctx", None)
    return jax.shard_map(
        body,
        mesh=mesh,
        in_specs=(split, split, split, split, P(), P(), P()),
        out_specs=(split, split, split, P(), P(), P()),
        check_vma=False,
    )
```

```python
import jax
import jax.numpy as jnp
from jax import lax
from jax.experimental import pallas as pl
from jax.experimental.pallas import tpu as pltpu
from jax.sharding import PartitionSpec as P

HEADS = 40
WIDTH = 64
STATE = 128
TAPS = 4
TOK = 128
SIG = HEADS * WIDTH
CH = SIG + 2 * STATE
BLOCKS = SIG // 128
CTX = 32
CHIPS = 16
DPS = 8
GROUPS = 4
GW = SIG // GROUPS
GB = GW // 128
HALF = STATE // 2
ROWS = 16
OWNERS = CH // 128
CUT_HALO = 4
CUT_PAIR = 10
CUT_SUMS = 3
CUT_BACK = 8
CUT_AHEAD = 14
VMEM = 48 * 1024 * 1024
LOG2E = 1.4426950408889634
F32 = jnp.float32
BF16 = jnp.bfloat16
MESH = pl.DeviceIdType.MESH


def dot(a, b, dims=((1,), (0,)), **kw):
    return lax.dot_general(a, b, (dims, ((), ())), preferred_element_type=F32, **kw)


def split3(v):
    hi = v.astype(BF16)
    rest = v - hi.astype(F32)
    mid = rest.astype(BF16)
    low = (rest - mid.astype(F32)).astype(BF16)
    return hi, mid, low


def loop(lo, hi, fn, unroll=1):
    whole = lo + (hi - lo) // unroll * unroll

    def step(i, carry):
        for k in range(unroll):
            fn(lo + i * unroll + k)
        return carry

    if whole > lo:
        lax.fori_loop(0, (whole - lo) // unroll, step, 0)
    for i in range(whole, hi):
        fn(jnp.int32(i))


def cols(i, width=128):
    return pl.ds(pl.multiple_of(i * width, 128), width)


def kernel(
    x_hbm, raw_hbm, ld_hbm, cot_hbm, w_hbm, b_hbm, skip_hbm,
    out_ref, gin_ref, sg_ref, wg_ref, bg_ref, kg_ref,
    xb, cot_ref, w_ref, b_ref, skip_ref, raw_ref,
    xe, halo, act, dsil, ldp, stp, dst, dsx, stx, fsx, tex, tail, gst, sst,
    loc, prt, dec, decp, decg, dcx, coef, skx, tsum, rcv, res, inc, snd, fin,
    oi, bi, run, tmp, xsh, gp, zhi, zlo, onehot, skp, part, ar1, ar2, sum1, tot,
    in_sem, h_sem, d_sem, dg_s, p1_s, p1_r, a_s, a_r, b_s, b_r, p2_s, p2_r, g_sem,
    r1_s, r2_s, r3_s,
):
    me = lax.axis_index("ctx")
    zed = lax.axis_index("dp")
    core = lax.rem(me, 2)
    chip = me // 2
    quarter = lax.rem(chip, 4)
    band = chip // 4
    mate = me + 1 - 2 * core
    nxt = lax.rem(me + 1, CTX)
    prv = lax.rem(me + CTX - 1, CTX)
    first = core == 0

    def send(src, dst, ssem, rsem, ctx):
        return pltpu.make_async_remote_copy(
            src_ref=src, dst_ref=dst, send_sem=ssem, recv_sem=rsem,
            device_id={"ctx": ctx}, device_id_type=MESH,
        )

    def left_all(ref, sem):
        send(ref, ref, sem, sem, mate).wait_send()

    def came_all(ref, sem):
        send(ref, ref, sem, sem, mate).wait_recv()

    def turned(i, own):
        away = jnp.where(i == 0, 2, jnp.where(i == 1, 1, jnp.where(i == 2, 3, 0)))
        return lax.rem(own + away, 4)

    def far_first(i):
        q = 4 * turned(i // 8, band) + turned(lax.rem(i // 2, 4), quarter)
        return 2 * q + lax.rem(core + 1 + i, 2)

    def far_dp(i):
        half = (i + 1) // 2
        return lax.rem(zed + 4 + jnp.where(lax.rem(i, 2) == 0, half, DPS - half), DPS)

    barrier = pltpu.get_barrier_semaphore()

    def greet_ctx(i):
        pl.semaphore_signal(
            barrier, inc=1, device_id={"ctx": lax.rem(me + i, CTX)}, device_id_type=MESH
        )

    def greet_dp(i):
        pl.semaphore_signal(
            barrier, inc=1, device_id={"dp": lax.rem(zed + i, DPS)}, device_id_type=MESH
        )

    fetch = [
        pltpu.make_async_copy(src, dst, in_sem.at[i])
        for i, (src, dst) in enumerate((
            (ld_hbm, ldp.at[pl.ds(0, HEADS), :]), (raw_hbm, raw_ref), (x_hbm, xb), (cot_hbm, cot_ref),
            (w_hbm, w_ref), (b_hbm, b_ref), (skip_hbm, skip_ref),
        ))
    ]
    for copy in fetch:
        copy.start()
    loop(1, CTX, greet_ctx)
    loop(1, DPS, greet_dp)

    rows = lax.broadcasted_iota(jnp.int32, (TOK, 128), 0)
    lanes = lax.broadcasted_iota(jnp.int32, (TOK, 128), 1)
    lower = rows >= lanes
    left = lanes < WIDTH

    ldp[HEADS:, :] = jnp.zeros((128 - HEADS, TOK), F32)
    stp[...] = jnp.zeros((128, TOK), F32)
    xe[0:8, :] = jnp.zeros((8, CH), F32)
    fetch[0].wait()

    ones = (rows <= lanes).astype(BF16)
    sums_t = sum(dot(v, ones) for v in split3(ldp[...] * LOG2E))
    dst[...] = sums_t
    sums = sums_t.T
    decay = jnp.exp2(sums[TOK - 1 : TOK, :])
    dec[...] = jnp.broadcast_to(decay, (8, 128))
    for copy in fetch[1:]:
        copy.wait()
    for g in range(BLOCKS):
        c = slice(128 * g, 128 * g + 128)
        pair = [jnp.broadcast_to(sums[:, h : h + 1], (TOK, 128)) for h in (2 * g, 2 * g + 1)]
        dsx[:, 256 * g : 256 * g + 128] = pair[0]
        dsx[:, 256 * g + 128 : 256 * g + 256] = pair[1]
        start = jnp.exp2(jnp.where(left, pair[0], pair[1]))
        fsx[:, c] = start
        gst[:, c] = (cot_ref[:, c].astype(F32) * start).astype(BF16)

    def expand(row, count):
        at = lax.broadcasted_iota(jnp.int32, (count, 128), 1) < WIDTH
        return [
            jnp.where(
                at,
                jnp.broadcast_to(row[:, 2 * g : 2 * g + 1], (count, 128)),
                jnp.broadcast_to(row[:, 2 * g + 1 : 2 * g + 2], (count, 128)),
            )
            for g in range(BLOCKS)
        ]

    def conv(j, r0, n):
        c = cols(j)
        pre = jnp.broadcast_to(b_ref[pl.ds(j, 1), :], (n, 128))
        for k in range(TAPS):
            moved = xe[5 + k + r0 : 5 + k + r0 + n, c]
            pre = pre + w_ref[k : k + 1, c] * moved
            if k < TAPS - 1:
                xsh[k, r0 : r0 + n, c] = moved
        sig = 1.0 / (1.0 + jnp.exp(-pre))
        act[r0 : r0 + n, c] = (pre * sig).astype(BF16)
        dsil[r0 : r0 + n, c] = sig * (1.0 + pre * (1.0 - sig))

    def ends(g):
        c = cols(g)
        ds = jnp.where(left, dsx[:, cols(2 * g)], dsx[:, cols(2 * g + 1)])
        tex[:, c] = jnp.exp2(ds[TOK - 1 : TOK, :] - ds)

    def scaled(g, r0, n):
        c = cols(g)
        r = slice(r0, r0 + n)
        s = act[r, c].astype(F32)
        step = stx[r, c]
        tail[r, c] = (s * (step * tex[r, c])).astype(BF16)
        sst[r, c] = (s * step).astype(BF16)

    def later_rows(j):
        c = cols(j)
        xe[8:, c] = xb[:, c].astype(F32)
        conv(j, ROWS, TOK - ROWS)

    def later_signal(g):
        later_rows(g)
        ends(g)
        scaled(g, ROWS, TOK - ROWS)

    loop(BLOCKS, BLOCKS + 2, later_rows)

    pl.semaphore_wait(barrier, CTX - 1 + DPS - 1)

    halo_copy = send(xb.at[pl.ds(TOK - 16, 16), :], halo, h_sem.at[0], h_sem.at[1], nxt)
    halo_copy.start()
    decay_copy = send(dec, decp, d_sem.at[0], d_sem.at[1], mate)
    decay_copy.start()

    raw = raw_ref[...]
    stp[0:HEADS, :] = jnp.maximum(raw, 0.0) + jnp.log1p(jnp.exp(-jnp.abs(raw)))
    steps = stp[...].T
    for g in range(BLOCKS):
        c = slice(128 * g, 128 * g + 128)
        stx[:, c] = jnp.where(
            left,
            jnp.broadcast_to(steps[:, 2 * g : 2 * g + 1], (TOK, 128)),
            jnp.broadcast_to(steps[:, 2 * g + 1 : 2 * g + 2], (TOK, 128)),
        )
    loop(0, CUT_HALO, later_signal, 2)

    decay_copy.wait()
    mine, other = dec[0:1, :], decp[0:1, :]
    decg[chip] = dec[...] * decp[...]

    def chip_at(i):
        return lax.rem(chip + i, CHIPS)

    def decay_out(q):
        return send(decg.at[chip], decg.at[chip], dg_s.at[0], dg_s.at[1], 2 * q + core)

    loop(1, CHIPS, lambda i: decay_out(chip_at(i)).start())
    for g, (a, b) in enumerate(zip(expand(mine, 1), expand(other, 1))):
        c = slice(128 * g, 128 * g + 128)
        coef[0:1, c] = a
        coef[1:2, c] = b

    halo_copy.wait_recv()
    xe[0:8, :] = jnp.where(me > 0, halo[...].astype(F32)[8:16, :], 0.0)
    loop(BLOCKS, BLOCKS + 2, lambda j: conv(j, 0, ROWS))
    inject = act[:, SIG : SIG + STATE]
    readout = act[:, SIG + STATE :]

    def pair_one(k, j):
        c = cols(j, GW)
        there = pl.ds(pl.multiple_of(HALF * (1 - core), HALF), HALF)
        return send(loc.at[k, there, c], prt.at[k, :, c], p1_s.at[k], p1_r.at[k, j], mate)

    readout_t = readout.T

    def local_adjoint(i):
        j = turned(i, quarter)
        c = cols(j, GW)
        loc[1, :, c] = dot(readout_t, gst[:, c]).astype(BF16)
        pair_one(1, j).start()

    loop(0, GROUPS, local_adjoint)

    inject_t = inject.T

    def local_state(i):
        j = turned(i, quarter)
        c = cols(j, GW)
        loc[0, :, c] = dot(inject_t, tail[:, c]).astype(BF16)
        pair_one(0, j).start()

    here = pl.ds(pl.multiple_of(HALF * core, HALF), HALF)
    own_rows = pl.ds(pl.multiple_of(ROWS * band, ROWS), ROWS)
    qc = cols(quarter, GW)

    def piece(ref, k, q):
        r = pl.ds(pl.multiple_of(ROWS * (q // 4), ROWS), ROWS)
        return ref.at[k, r, cols(lax.rem(q, 4), GW)]

    def state_out(k, q):
        return send(piece(tsum, k, q), rcv.at[k, chip], a_s.at[k], a_r.at[k], 2 * q + core)

    def chip_sums(k):
        def group(i):
            j = turned(i, quarter)
            pair_one(k, j).wait_recv()
            c = cols(j, GW)
            a, b = coef[0:1, c], coef[1:2, c]
            own = loc[k, here, c].astype(F32)
            far = prt[k, :, c].astype(F32)
            if k == 0:
                total = jnp.where(first, b * own + far, a * far + own)
            else:
                total = jnp.where(first, a * far + own, b * own + far)
            tsum[k, :, c] = total.astype(BF16)

            def out(r):
                q = 4 * turned(r, band) + j

                @pl.when(q != chip)
                def _():
                    state_out(k, q).start()

            loop(0, 4, out)

        loop(0, GROUPS, group)
        rcv[k, chip] = tsum[k, own_rows, qc]

    def early_rows(g):
        conv(g, 0, ROWS)
        scaled(g, 0, ROWS)

    loop(CUT_HALO, CUT_PAIR, later_signal, 2)
    chip_sums(1)
    loop(CUT_PAIR, BLOCKS, later_signal, 2)
    loop(0, BLOCKS, early_rows, 2)
    loop(0, GROUPS, local_state)

    scores = dot(readout, inject, ((1,), (1,)))
    scores_t = dot(inject, readout, ((1,), (1,)))
    low_scores = jnp.where(lower, scores, 0.0)
    up_scores = jnp.where(rows <= lanes, scores_t, 0.0)
    run[...] = jnp.zeros((TOK, 128), F32)
    lane_a = left.astype(BF16)
    lane_b = (lanes >= WIDTH).astype(BF16)

    def intra(g):
        c = cols(g)
        fades = []
        for e in range(2):
            gap = dsx[:, cols(2 * g + e)] - dst[pl.ds(2 * g + e, 1), :]
            fades.append(jnp.exp2(jnp.where(lower, gap, -gap)))
        mix = jnp.concatenate([(f * low_scores).astype(BF16) for f in fades], axis=1)
        mix_t = jnp.concatenate([(f * up_scores).astype(BF16) for f in fades], axis=1)
        s = sst[:, c]
        t = cot_ref[:, c]
        both = jnp.concatenate([s * lane_a, s * lane_b], axis=0)
        oi[:, c] = dot(mix, both)
        bi[:, c] = dot(mix_t, jnp.concatenate([t * lane_a, t * lane_b], axis=0))
        inner = dot(t, both, ((1,), (1,)))
        run[...] += fades[0] * inner[:, :128] + fades[1] * inner[:, 128:]
        skp[:, c] = jnp.sum((act[:, c].astype(F32) * t.astype(F32)).reshape(TOK // 8, 8, 128), axis=0)

    loop(0, CUT_SUMS, intra, 2)
    chip_sums(0)
    for g, v in enumerate(expand(skip_ref[...], 1)):
        skx[:, 128 * g : 128 * g + 128] = v
        onehot[128 * g : 128 * g + 128, :] = (
            lanes == 2 * g + (rows >= WIDTH).astype(jnp.int32)
        ).astype(BF16)
    loop(CUT_SUMS, CUT_BACK, intra, 2)

    came_all(decg.at[pl.ds(0, CHIPS - 1)], dg_s.at[1])
    for g, v in enumerate(expand(decg[:, 0, :], CHIPS)):
        dcx[:, 128 * g : 128 * g + 128] = v

    def result_out(k, q):
        return send(res.at[k, q], piece(inc, k, chip), b_s.at[k], b_r.at[k, quarter], 2 * q + core)

    def scan(k):
        came_all(rcv.at[k, pl.ds(0, CHIPS - 1)], a_r.at[k])

        def step(i, carry):
            q = i if k == 0 else CHIPS - 1 - i
            res[k, q] = carry.astype(BF16)
            return dcx[pl.ds(q, 1), qc] * carry + rcv[k, q].astype(F32)

        lax.fori_loop(0, CHIPS, step, jnp.zeros((ROWS, GW), F32))

        def out(i):
            q = 4 * turned(i // 4, band) + turned(lax.rem(i, 4), quarter)
            result_out(k, q).start()

        loop(0, CHIPS - 1, out)
        inc[k, own_rows, qc] = res[k, chip]

    scan(1)
    loop(CUT_BACK, CUT_AHEAD, intra, 2)
    scan(0)
    loop(CUT_AHEAD, BLOCKS, intra, 2)

    skip_heads = sum(dot(v, onehot[...]) for v in split3(skp[...]))
    mix_total = jnp.where(lower, run[...], 0.0).astype(BF16)
    grad_readout = dot(mix_total, inject)
    grad_inject = dot(mix_total.T, readout)
    part[...] = jnp.zeros((8, CH), F32)
    part[5:6, 0:128] = jnp.sum(skip_heads, axis=0, keepdims=True)

    def pair_two(k, j):
        c = cols(j, GW)
        return send(snd.at[k, :, c], fin.at[k, here, c], p2_s.at[k], p2_r.at[k, j], mate)

    def spread(k):
        def group(i):
            j = lax.rem(quarter + i, 4)
            c = cols(j, GW)

            @pl.when(j == quarter)
            def _():
                came_all(inc.at[k, pl.ds(0, HALF - ROWS), c], b_r.at[k, j])

            @pl.when(j != quarter)
            def _():
                came_all(inc.at[k, :, c], b_r.at[k, j])

            came = inc[k, :, c]
            wide = came.astype(F32)
            near = (coef[0:1, c] * wide + loc[k, here, c].astype(F32)).astype(BF16)
            far = (coef[1:2, c] * wide + prt[k, :, c].astype(F32)).astype(BF16)
            if k == 0:
                snd[k, :, c] = jnp.where(first, near, came)
                fin[k, here, c] = jnp.where(first, came, far)
            else:
                snd[k, :, c] = jnp.where(first, came, near)
                fin[k, here, c] = jnp.where(first, far, came)
            pair_two(k, j).start()

        loop(0, GROUPS, group)

    spread(1)

    def tile_out(j):
        return send(part.at[:, cols(j)], ar1.at[me], r1_s.at[0], r1_s.at[1], j)

    def each_other(i, fn):
        @pl.when(i != me)
        def _():
            fn(i)

    def finish_rows(j, grad_act):
        c = cols(j)
        grad = grad_act * dsil[:, c]
        gp[0:TOK, c] = grad
        for k in range(TAPS):
            moved = xe[8:, c] if k == TAPS - 1 else xsh[k, :, c]
            part[k : k + 1, c] = jnp.sum(grad * moved, axis=0, keepdims=True)
        part[4:5, c] = jnp.sum(grad, axis=0, keepdims=True)

    def finish(g, i):
        c = cols(g)
        s = act[:, c].astype(F32)
        t = cot_ref[:, c].astype(F32)
        back = bi[:, c] + tex[:, c] * tmp[:, cols(i)]
        z = s * back
        z_hi = z.astype(BF16)
        zhi[:, c] = z_hi
        zlo[:, c] = (z - z_hi.astype(F32)).astype(BF16)
        finish_rows(g, stx[:, c] * back + skx[:, c] * t)

    def finish_group(i):
        j = lax.rem(quarter + i, 4)
        pair_two(1, j).wait_recv()
        tmp[...] = dot(inject, fin[1, :, cols(j, GW)])
        loop(0, GB, lambda i: finish(j * GB + i, i), GB)
        loop(0, GB, lambda i: each_other(j * GB + i, lambda t: tile_out(t).start()))

    loop(0, GROUPS, finish_group)
    finish_rows(BLOCKS, grad_inject + dot(tail[...], fin[1], ((1,), (1,))))
    each_other(BLOCKS, lambda j: tile_out(j).start())
    spread(0)
    loop(0, GROUPS, lambda j: pair_two(0, j).wait_recv())
    finish_rows(BLOCKS + 1, grad_readout + dot(gst[...], fin[0], ((1,), (1,))))
    each_other(OWNERS - 1, lambda j: tile_out(j).start())

    grad_halo = send(gp.at[pl.ds(0, 8), :], gp.at[pl.ds(TOK, 8), :], g_sem.at[0], g_sem.at[1], prv)
    grad_halo.start()

    def output(g, i):
        c = cols(g)
        out = oi[:, c] + fsx[:, c] * tmp[:, cols(i)] + skx[:, c] * act[:, c].astype(F32)
        out_ref[:, c] = out.astype(BF16)

    def output_group(j):
        tmp[...] = dot(readout, fin[0, :, cols(j, GW)])
        loop(0, GB, lambda i: output(j * GB + i, i))

    loop(0, GROUPS, output_group)

    def dp_out(i):
        z = far_dp(i)
        return pltpu.make_async_remote_copy(
            src_ref=sum1, dst_ref=ar2.at[zed], send_sem=r2_s.at[0], recv_sem=r2_s.at[1],
            device_id={"dp": z}, device_id_type=MESH,
        )

    def total_out(i):
        return send(tot.at[:, cols(me)], tot.at[:, cols(me)], r3_s.at[0], r3_s.at[1], i)

    owner = me < OWNERS

    @pl.when(owner)
    def _():
        came_all(ar1.at[pl.ds(0, CTX - 1)], r1_s.at[1])
        ar1[me] = part[:, cols(me)]
        sum1[...] = jnp.sum(ar1[...], axis=0)
        loop(0, DPS - 1, lambda i: dp_out(i).start())

    steps_z = dot(zhi[...], onehot[...]) + dot(zlo[...], onehot[...])
    e = jnp.exp(-jnp.abs(raw))
    gate = jnp.where(raw >= 0, 1.0, e) / (1.0 + e)
    sg_ref[...] = steps_z.T[0:HEADS, :] * gate

    grad_halo.wait_recv()
    gp[TOK:, :] = jnp.where(me < CTX - 1, gp[TOK:, :], 0.0)

    def input_grad(j):
        c = cols(j)
        total = w_ref[0:1, c] * gp[3 : 3 + TOK, c]
        for k in range(1, TAPS):
            total = total + w_ref[k : k + 1, c] * gp[3 - k : 3 - k + TOK, c]
        gin_ref[:, c] = total.astype(BF16)

    loop(0, CH // 256, input_grad)

    @pl.when(owner)
    def _():
        came_all(ar2.at[pl.ds(0, DPS - 1)], r2_s.at[1])
        ar2[zed] = sum1[...]
        tot[:, cols(me)] = jnp.sum(ar2[...], axis=0)
        loop(0, CTX - 1, lambda i: total_out(far_first(i)).start())

    loop(CH // 256, CH // 128, input_grad)

    halo_copy.wait_send()
    grad_halo.wait_send()

    left_all(decg.at[pl.ds(0, CHIPS - 1)], dg_s.at[0])
    for k in range(2):
        left_all(tsum.at[k], p1_s.at[k])
        left_all(tsum.at[k], p2_s.at[k])
        left_all(rcv.at[k, pl.ds(0, CHIPS - 1)], a_s.at[k])
        left_all(rcv.at[k, pl.ds(0, CHIPS - 1)], b_s.at[k])

    @pl.when(owner)
    def _():
        some = tot.at[:, pl.ds(0, CH - 128)]
        left_all(some, r1_s.at[0])
        left_all(ar2.at[pl.ds(0, DPS - 1)], r2_s.at[0])
        left_all(ar1.at[pl.ds(0, CTX - 1)], r3_s.at[0])
        came_all(some, r3_s.at[1])

    @pl.when(jnp.logical_not(owner))
    def _():
        left_all(tot, r1_s.at[0])
        came_all(tot, r3_s.at[1])

    wg_ref[...] = tot[0:TAPS, :]
    for j in range(OWNERS):
        bg_ref[j : j + 1, :] = tot[4:5, 128 * j : 128 * j + 128]
    kg_ref[...] = tot[5:6, 0:HEADS]


def copy_kernel(*refs):
    n = len(refs) // 2
    copies = [pltpu.make_async_copy(refs[i], refs[n + i], refs[-1].at[i]) for i in range(n)]
    for copy in copies:
        copy.start()
    for copy in copies:
        copy.wait()


def scratch():
    v = pltpu.VMEM
    dma = pltpu.SemaphoreType.DMA
    return [
        v((TOK, CH), BF16),
        v((TOK, SIG), BF16),
        v((TAPS, CH), F32),
        v((OWNERS, 128), F32),
        v((1, HEADS), F32),
        v((HEADS, TOK), F32),
        v((TOK + 8, CH), F32),
        v((16, CH), BF16),
        v((TOK, CH), BF16),
        v((TOK, CH), F32),
        v((128, TOK), F32),
        v((128, TOK), F32),
        v((128, TOK), F32),
        v((TOK, HEADS * 128), F32),
        v((TOK, SIG), F32),
        v((TOK, SIG), F32),
        v((TOK, SIG), F32),
        v((TOK, SIG), BF16),
        v((TOK, SIG), BF16),
        v((TOK, SIG), BF16),
        v((2, STATE, SIG), BF16),
        v((2, HALF, SIG), BF16),
        v((8, 128), F32),
        v((8, 128), F32),
        v((CHIPS, 8, 128), F32),
        v((CHIPS, SIG), F32),
        v((8, SIG), F32),
        v((1, SIG), F32),
        v((2, HALF, SIG), BF16),
        v((2, CHIPS, ROWS, GW), BF16),
        v((2, CHIPS, ROWS, GW), BF16),
        v((2, HALF, SIG), BF16),
        v((2, HALF, SIG), BF16),
        v((2, STATE, SIG), BF16),
        v((TOK, SIG), F32),
        v((TOK, SIG), F32),
        v((TOK, 128), F32),
        v((TOK, GW), F32),
        v((TAPS - 1, TOK, CH), F32),
        v((TOK + 8, CH), F32),
        v((TOK, SIG), BF16),
        v((TOK, SIG), BF16),
        v((SIG, 128), BF16),
        v((8, SIG), F32),
        v((8, CH), F32),
        v((CTX, 8, 128), F32),
        v((DPS, 8, 128), F32),
        v((8, 128), F32),
        v((8, CH), F32),
        dma((7,)),
        dma((2,)),
        dma((2,)),
        dma((2,)),
        dma((2,)),
        dma((2, GROUPS)),
        dma((2,)),
        dma((2,)),
        dma((2,)),
        dma((2, GROUPS)),
        dma((2,)),
        dma((2, GROUPS)),
        dma((2,)),
        dma((2,)),
        dma((2,)),
        dma((2,)),
    ]


def body(conv_input, step_raw, log_decay, cotangent, conv_weight, conv_bias, skip_gain):
    vmem = pl.BlockSpec(memory_space=pltpu.VMEM)
    hbm = pl.BlockSpec(memory_space=pltpu.HBM)
    shapes = (
        jax.ShapeDtypeStruct((TOK, SIG), BF16),
        jax.ShapeDtypeStruct((TOK, CH), BF16),
        jax.ShapeDtypeStruct((HEADS, TOK), F32),
        jax.ShapeDtypeStruct((TAPS, CH), F32),
        jax.ShapeDtypeStruct((OWNERS, 128), F32),
        jax.ShapeDtypeStruct((1, HEADS), F32),
    )
    results = pl.pallas_call(
        kernel,
        out_shape=[pltpu.VMEM(a.shape, a.dtype) for a in shapes],
        in_specs=[hbm] * 7,
        out_specs=[vmem] * 6,
        scratch_shapes=scratch(),
        compiler_params=pltpu.CompilerParams(
            collective_id=0, has_side_effects=True, vmem_limit_bytes=VMEM
        ),
    )(*(pltpu.with_memory_space_constraint(a, pltpu.HBM) for a in (
        conv_input[0], step_raw[0].T, log_decay[0].T, cotangent[0],
        conv_weight, conv_bias.reshape(OWNERS, 128), skip_gain[None],
    )))
    out, gin, sg, wg, bg, kg = pl.pallas_call(
        copy_kernel,
        out_shape=shapes,
        in_specs=[vmem] * 6,
        out_specs=[hbm] * 6,
        scratch_shapes=[pltpu.SemaphoreType.DMA((6,))],
    )(*(pltpu.with_memory_space_constraint(a, pltpu.VMEM) for a in results))
    return out[None], gin[None], sg.T[None], wg, bg.reshape(CH), kg[0]


def solution(mesh):
    split = P("dp", "ctx", None)
    return jax.shard_map(
        body,
        mesh=mesh,
        in_specs=(split, split, split, split, P(), P(), P()),
        out_specs=(split, split, split, P(), P(), P()),
        check_vma=False,
    )
```

```python
import jax
import jax.numpy as jnp
from jax import lax
from jax.experimental import pallas as pl
from jax.experimental.pallas import tpu as pltpu
from jax.sharding import PartitionSpec as P

HEADS = 40
WIDTH = 64
STATE = 128
TAPS = 4
TOK = 128
SIG = HEADS * WIDTH
CH = SIG + 2 * STATE
BLOCKS = SIG // 128
CTX = 32
CHIPS = 16
DPS = 8
GROUPS = 4
GW = SIG // GROUPS
GB = GW // 128
HALF = STATE // 2
ROWS = 16
OWNERS = CH // 128
CUT_HALO = 4
CUT_PAIR = 10
CUT_SUMS = 3
CUT_BACK = 8
CUT_AHEAD = 14
VMEM = 48 * 1024 * 1024
LOG2E = 1.4426950408889634
F32 = jnp.float32
BF16 = jnp.bfloat16
MESH = pl.DeviceIdType.MESH


def dot(a, b, dims=((1,), (0,)), **kw):
    return lax.dot_general(a, b, (dims, ((), ())), preferred_element_type=F32, **kw)


def split3(v):
    hi = v.astype(BF16)
    rest = v - hi.astype(F32)
    mid = rest.astype(BF16)
    low = (rest - mid.astype(F32)).astype(BF16)
    return hi, mid, low


def loop(lo, hi, fn, unroll=1):
    whole = lo + (hi - lo) // unroll * unroll

    def step(i, carry):
        for k in range(unroll):
            fn(lo + i * unroll + k)
        return carry

    if whole > lo:
        lax.fori_loop(0, (whole - lo) // unroll, step, 0)
    for i in range(whole, hi):
        fn(jnp.int32(i))


def cols(i, width=128):
    return pl.ds(pl.multiple_of(i * width, 128), width)


def kernel(
    x_hbm, raw_hbm, ld_hbm, cot_hbm, w_hbm, b_hbm, skip_hbm,
    out_ref, gin_ref, sg_ref, wg_ref, bg_ref, kg_ref,
    xb, cot_ref, w_ref, b_ref, skip_ref, raw_ref,
    xe, halo, act, dsil, ldp, stp, dst, dsx, stx, fsx, tex, tail, gst, sst,
    loc, prt, dec, decp, decg, dcx, coef, skx, tsum, rcv, res, inc, snd, fin,
    oi, bi, run, tmp, xsh, gp, zhi, zlo, onehot, skp, part, ar1, ar2, sum1, tot,
    in_sem, h_sem, d_sem, dg_s, p1_s, p1_r, a_s, a_r, b_s, b_r, p2_s, p2_r, g_sem,
    r1_s, r2_s, r3_s,
):
    me = lax.axis_index("ctx")
    zed = lax.axis_index("dp")
    core = lax.rem(me, 2)
    chip = me // 2
    quarter = lax.rem(chip, 4)
    band = chip // 4
    mate = me + 1 - 2 * core
    nxt = lax.rem(me + 1, CTX)
    prv = lax.rem(me + CTX - 1, CTX)
    first = core == 0

    def send(src, dst, ssem, rsem, ctx):
        return pltpu.make_async_remote_copy(
            src_ref=src, dst_ref=dst, send_sem=ssem, recv_sem=rsem,
            device_id={"ctx": ctx}, device_id_type=MESH,
        )

    def left_all(ref, sem):
        send(ref, ref, sem, sem, mate).wait_send()

    def came_all(ref, sem):
        send(ref, ref, sem, sem, mate).wait_recv()

    def turned(i, own):
        away = jnp.where(i == 0, 2, jnp.where(i == 1, 1, jnp.where(i == 2, 3, 0)))
        return lax.rem(own + away, 4)

    def far_first(i):
        q = 4 * turned(i // 8, band) + turned(lax.rem(i // 2, 4), quarter)
        return 2 * q + lax.rem(core + 1 + i, 2)

    def far_dp(i):
        half = (i + 1) // 2
        return lax.rem(zed + 4 + jnp.where(lax.rem(i, 2) == 0, half, DPS - half), DPS)

    barrier = pltpu.get_barrier_semaphore()

    def greet_ctx(i):
        pl.semaphore_signal(
            barrier, inc=1, device_id={"ctx": lax.rem(me + i, CTX)}, device_id_type=MESH
        )

    def greet_dp(i):
        pl.semaphore_signal(
            barrier, inc=1, device_id={"dp": lax.rem(zed + i, DPS)}, device_id_type=MESH
        )

    fetch = [
        pltpu.make_async_copy(src, dst, in_sem.at[i])
        for i, (src, dst) in enumerate((
            (ld_hbm, ldp.at[pl.ds(0, HEADS), :]), (cot_hbm, cot_ref), (x_hbm, xb), (raw_hbm, raw_ref),
            (w_hbm, w_ref), (b_hbm, b_ref), (skip_hbm, skip_ref),
        ))
    ]
    for copy in fetch:
        copy.start()
    loop(1, CTX, greet_ctx)
    loop(1, DPS, greet_dp)

    rows = lax.broadcasted_iota(jnp.int32, (TOK, 128), 0)
    lanes = lax.broadcasted_iota(jnp.int32, (TOK, 128), 1)
    lower = rows >= lanes
    left = lanes < WIDTH

    ldp[HEADS:, :] = jnp.zeros((128 - HEADS, TOK), F32)
    stp[...] = jnp.zeros((128, TOK), F32)
    xe[0:8, :] = jnp.zeros((8, CH), F32)
    fetch[0].wait()

    ones = (rows <= lanes).astype(BF16)
    sums_t = sum(dot(v, ones) for v in split3(ldp[...] * LOG2E))
    dst[...] = sums_t
    sums = sums_t.T
    decay = jnp.exp2(sums[TOK - 1 : TOK, :])
    dec[...] = jnp.broadcast_to(decay, (8, 128))
    fetch[1].wait()
    for g in range(BLOCKS):
        c = slice(128 * g, 128 * g + 128)
        pair = [jnp.broadcast_to(sums[:, h : h + 1], (TOK, 128)) for h in (2 * g, 2 * g + 1)]
        dsx[:, 256 * g : 256 * g + 128] = pair[0]
        dsx[:, 256 * g + 128 : 256 * g + 256] = pair[1]
        start = jnp.exp2(jnp.where(left, pair[0], pair[1]))
        fsx[:, c] = start
        gst[:, c] = (cot_ref[:, c].astype(F32) * start).astype(BF16)

    def expand(row, count):
        at = lax.broadcasted_iota(jnp.int32, (count, 128), 1) < WIDTH
        return [
            jnp.where(
                at,
                jnp.broadcast_to(row[:, 2 * g : 2 * g + 1], (count, 128)),
                jnp.broadcast_to(row[:, 2 * g + 1 : 2 * g + 2], (count, 128)),
            )
            for g in range(BLOCKS)
        ]

    def conv(j, r0, n):
        c = cols(j)
        pre = jnp.broadcast_to(b_ref[pl.ds(j, 1), :], (n, 128))
        for k in range(TAPS):
            moved = xe[5 + k + r0 : 5 + k + r0 + n, c]
            pre = pre + w_ref[k : k + 1, c] * moved
            if k < TAPS - 1:
                xsh[k, r0 : r0 + n, c] = moved
        sig = 1.0 / (1.0 + jnp.exp(-pre))
        act[r0 : r0 + n, c] = (pre * sig).astype(BF16)
        dsil[r0 : r0 + n, c] = sig * (1.0 + pre * (1.0 - sig))

    def ends(g):
        c = cols(g)
        ds = jnp.where(left, dsx[:, cols(2 * g)], dsx[:, cols(2 * g + 1)])
        tex[:, c] = jnp.exp2(ds[TOK - 1 : TOK, :] - ds)

    def scaled(g, r0, n):
        c = cols(g)
        r = slice(r0, r0 + n)
        s = act[r, c].astype(F32)
        step = stx[r, c]
        tail[r, c] = (s * (step * tex[r, c])).astype(BF16)
        sst[r, c] = (s * step).astype(BF16)

    def later_rows(j):
        c = cols(j)
        xe[8:, c] = xb[:, c].astype(F32)
        conv(j, ROWS, TOK - ROWS)

    def later_signal(g):
        later_rows(g)
        ends(g)
        scaled(g, ROWS, TOK - ROWS)

    for copy in fetch[2:]:
        copy.wait()
    loop(BLOCKS, BLOCKS + 2, later_rows)

    pl.semaphore_wait(barrier, CTX - 1 + DPS - 1)

    halo_copy = send(xb.at[pl.ds(TOK - 16, 16), :], halo, h_sem.at[0], h_sem.at[1], nxt)
    halo_copy.start()
    decay_copy = send(dec, decp, d_sem.at[0], d_sem.at[1], mate)
    decay_copy.start()

    raw = raw_ref[...]
    stp[0:HEADS, :] = jnp.maximum(raw, 0.0) + jnp.log1p(jnp.exp(-jnp.abs(raw)))
    steps = stp[...].T
    for g in range(BLOCKS):
        c = slice(128 * g, 128 * g + 128)
        stx[:, c] = jnp.where(
            left,
            jnp.broadcast_to(steps[:, 2 * g : 2 * g + 1], (TOK, 128)),
            jnp.broadcast_to(steps[:, 2 * g + 1 : 2 * g + 2], (TOK, 128)),
        )
    loop(0, CUT_HALO, later_signal, 2)

    decay_copy.wait()
    mine, other = dec[0:1, :], decp[0:1, :]
    decg[chip] = dec[...] * decp[...]

    def chip_at(i):
        return lax.rem(chip + i, CHIPS)

    def decay_out(q):
        return send(decg.at[chip], decg.at[chip], dg_s.at[0], dg_s.at[1], 2 * q + core)

    loop(1, CHIPS, lambda i: decay_out(chip_at(i)).start())
    for g, (a, b) in enumerate(zip(expand(mine, 1), expand(other, 1))):
        c = slice(128 * g, 128 * g + 128)
        coef[0:1, c] = a
        coef[1:2, c] = b

    halo_copy.wait_recv()
    xe[0:8, :] = jnp.where(me > 0, halo[...].astype(F32)[8:16, :], 0.0)
    loop(BLOCKS, BLOCKS + 2, lambda j: conv(j, 0, ROWS))
    inject = act[:, SIG : SIG + STATE]
    readout = act[:, SIG + STATE :]

    def pair_one(k, j):
        c = cols(j, GW)
        there = pl.ds(pl.multiple_of(HALF * (1 - core), HALF), HALF)
        return send(loc.at[k, there, c], prt.at[k, :, c], p1_s.at[k], p1_r.at[k, j], mate)

    readout_t = readout.T

    def local_adjoint(i):
        j = turned(i, quarter)
        c = cols(j, GW)
        loc[1, :, c] = dot(readout_t, gst[:, c]).astype(BF16)
        pair_one(1, j).start()

    loop(0, GROUPS, local_adjoint)

    inject_t = inject.T

    def local_state(i):
        j = turned(i, quarter)
        c = cols(j, GW)
        loc[0, :, c] = dot(inject_t, tail[:, c]).astype(BF16)
        pair_one(0, j).start()

    here = pl.ds(pl.multiple_of(HALF * core, HALF), HALF)
    own_rows = pl.ds(pl.multiple_of(ROWS * band, ROWS), ROWS)
    qc = cols(quarter, GW)

    def piece(ref, k, q):
        r = pl.ds(pl.multiple_of(ROWS * (q // 4), ROWS), ROWS)
        return ref.at[k, r, cols(lax.rem(q, 4), GW)]

    def state_out(k, q):
        return send(piece(tsum, k, q), rcv.at[k, chip], a_s.at[k], a_r.at[k], 2 * q + core)

    def chip_sums(k):
        def group(i):
            j = turned(i, quarter)
            pair_one(k, j).wait_recv()
            c = cols(j, GW)
            a, b = coef[0:1, c], coef[1:2, c]
            own = loc[k, here, c].astype(F32)
            far = prt[k, :, c].astype(F32)
            if k == 0:
                total = jnp.where(first, b * own + far, a * far + own)
            else:
                total = jnp.where(first, a * far + own, b * own + far)
            tsum[k, :, c] = total.astype(BF16)

            def out(r):
                q = 4 * turned(r, band) + j

                @pl.when(q != chip)
                def _():
                    state_out(k, q).start()

            loop(0, 4, out)

        loop(0, GROUPS, group)
        rcv[k, chip] = tsum[k, own_rows, qc]

    def early_rows(g):
        conv(g, 0, ROWS)
        scaled(g, 0, ROWS)

    loop(CUT_HALO, CUT_PAIR, later_signal, 2)
    chip_sums(1)
    loop(CUT_PAIR, BLOCKS, later_signal, 2)
    loop(0, BLOCKS, early_rows, 2)
    loop(0, GROUPS, local_state)

    scores = dot(readout, inject, ((1,), (1,)))
    scores_t = dot(inject, readout, ((1,), (1,)))
    low_scores = jnp.where(lower, scores, 0.0)
    up_scores = jnp.where(rows <= lanes, scores_t, 0.0)
    run[...] = jnp.zeros((TOK, 128), F32)
    lane_a = left.astype(BF16)
    lane_b = (lanes >= WIDTH).astype(BF16)

    def intra(g):
        c = cols(g)
        fades = []
        for e in range(2):
            gap = dsx[:, cols(2 * g + e)] - dst[pl.ds(2 * g + e, 1), :]
            fades.append(jnp.exp2(jnp.where(lower, gap, -gap)))
        mix = jnp.concatenate([(f * low_scores).astype(BF16) for f in fades], axis=1)
        mix_t = jnp.concatenate([(f * up_scores).astype(BF16) for f in fades], axis=1)
        s = sst[:, c]
        t = cot_ref[:, c]
        both = jnp.concatenate([s * lane_a, s * lane_b], axis=0)
        oi[:, c] = dot(mix, both)
        bi[:, c] = dot(mix_t, jnp.concatenate([t * lane_a, t * lane_b], axis=0))
        inner = dot(t, both, ((1,), (1,)))
        run[...] += fades[0] * inner[:, :128] + fades[1] * inner[:, 128:]
        skp[:, c] = jnp.sum((act[:, c].astype(F32) * t.astype(F32)).reshape(TOK // 8, 8, 128), axis=0)

    loop(0, CUT_SUMS, intra, 2)
    chip_sums(0)
    for g, v in enumerate(expand(skip_ref[...], 1)):
        skx[:, 128 * g : 128 * g + 128] = v
        onehot[128 * g : 128 * g + 128, :] = (
            lanes == 2 * g + (rows >= WIDTH).astype(jnp.int32)
        ).astype(BF16)
    loop(CUT_SUMS, CUT_BACK, intra, 2)

    came_all(decg.at[pl.ds(0, CHIPS - 1)], dg_s.at[1])
    for g, v in enumerate(expand(decg[:, 0, :], CHIPS)):
        dcx[:, 128 * g : 128 * g + 128] = v

    def result_out(k, q):
        return send(res.at[k, q], piece(inc, k, chip), b_s.at[k], b_r.at[k, quarter], 2 * q + core)

    def scan(k):
        came_all(rcv.at[k, pl.ds(0, CHIPS - 1)], a_r.at[k])

        def step(i, carry):
            q = i if k == 0 else CHIPS - 1 - i
            res[k, q] = carry.astype(BF16)
            return dcx[pl.ds(q, 1), qc] * carry + rcv[k, q].astype(F32)

        lax.fori_loop(0, CHIPS, step, jnp.zeros((ROWS, GW), F32))

        def out(i):
            q = 4 * turned(i // 4, band) + turned(lax.rem(i, 4), quarter)
            result_out(k, q).start()

        loop(0, CHIPS - 1, out)
        inc[k, own_rows, qc] = res[k, chip]

    scan(1)
    loop(CUT_BACK, CUT_AHEAD, intra, 2)
    scan(0)
    loop(CUT_AHEAD, BLOCKS, intra, 2)

    skip_heads = sum(dot(v, onehot[...]) for v in split3(skp[...]))
    mix_total = jnp.where(lower, run[...], 0.0).astype(BF16)
    grad_readout = dot(mix_total, inject)
    grad_inject = dot(mix_total.T, readout)
    part[...] = jnp.zeros((8, CH), F32)
    part[5:6, 0:128] = jnp.sum(skip_heads, axis=0, keepdims=True)

    def pair_two(k, j):
        c = cols(j, GW)
        return send(snd.at[k, :, c], fin.at[k, here, c], p2_s.at[k], p2_r.at[k, j], mate)

    def spread(k):
        def group(i):
            j = lax.rem(quarter + i, 4)
            c = cols(j, GW)

            @pl.when(j == quarter)
            def _():
                came_all(inc.at[k, pl.ds(0, HALF - ROWS), c], b_r.at[k, j])

            @pl.when(j != quarter)
            def _():
                came_all(inc.at[k, :, c], b_r.at[k, j])

            came = inc[k, :, c]
            wide = came.astype(F32)
            near = (coef[0:1, c] * wide + loc[k, here, c].astype(F32)).astype(BF16)
            far = (coef[1:2, c] * wide + prt[k, :, c].astype(F32)).astype(BF16)
            if k == 0:
                snd[k, :, c] = jnp.where(first, near, came)
                fin[k, here, c] = jnp.where(first, came, far)
            else:
                snd[k, :, c] = jnp.where(first, came, near)
                fin[k, here, c] = jnp.where(first, far, came)
            pair_two(k, j).start()

        loop(0, GROUPS, group)

    spread(1)

    def tile_out(j):
        return send(part.at[:, cols(j)], ar1.at[me], r1_s.at[0], r1_s.at[1], j)

    def each_other(i, fn):
        @pl.when(i != me)
        def _():
            fn(i)

    def finish_rows(j, grad_act):
        c = cols(j)
        grad = grad_act * dsil[:, c]
        gp[0:TOK, c] = grad
        for k in range(TAPS):
            moved = xe[8:, c] if k == TAPS - 1 else xsh[k, :, c]
            part[k : k + 1, c] = jnp.sum(grad * moved, axis=0, keepdims=True)
        part[4:5, c] = jnp.sum(grad, axis=0, keepdims=True)

    def finish(g, i):
        c = cols(g)
        s = act[:, c].astype(F32)
        t = cot_ref[:, c].astype(F32)
        back = bi[:, c] + tex[:, c] * tmp[:, cols(i)]
        z = s * back
        z_hi = z.astype(BF16)
        zhi[:, c] = z_hi
        zlo[:, c] = (z - z_hi.astype(F32)).astype(BF16)
        finish_rows(g, stx[:, c] * back + skx[:, c] * t)

    def finish_group(i):
        j = lax.rem(quarter + i, 4)
        pair_two(1, j).wait_recv()
        tmp[...] = dot(inject, fin[1, :, cols(j, GW)])
        loop(0, GB, lambda i: finish(j * GB + i, i), GB)
        loop(0, GB, lambda i: each_other(j * GB + i, lambda t: tile_out(t).start()))

    loop(0, GROUPS, finish_group)
    finish_rows(BLOCKS, grad_inject + dot(tail[...], fin[1], ((1,), (1,))))
    each_other(BLOCKS, lambda j: tile_out(j).start())
    spread(0)
    loop(0, GROUPS, lambda j: pair_two(0, j).wait_recv())
    finish_rows(BLOCKS + 1, grad_readout + dot(gst[...], fin[0], ((1,), (1,))))
    each_other(OWNERS - 1, lambda j: tile_out(j).start())

    grad_halo = send(gp.at[pl.ds(0, 8), :], gp.at[pl.ds(TOK, 8), :], g_sem.at[0], g_sem.at[1], prv)
    grad_halo.start()

    def output(g, i):
        c = cols(g)
        out = oi[:, c] + fsx[:, c] * tmp[:, cols(i)] + skx[:, c] * act[:, c].astype(F32)
        out_ref[:, c] = out.astype(BF16)

    def output_group(j):
        tmp[...] = dot(readout, fin[0, :, cols(j, GW)])
        loop(0, GB, lambda i: output(j * GB + i, i))

    loop(0, GROUPS, output_group)

    def dp_out(i):
        z = far_dp(i)
        return pltpu.make_async_remote_copy(
            src_ref=sum1, dst_ref=ar2.at[zed], send_sem=r2_s.at[0], recv_sem=r2_s.at[1],
            device_id={"dp": z}, device_id_type=MESH,
        )

    def total_out(i):
        return send(tot.at[:, cols(me)], tot.at[:, cols(me)], r3_s.at[0], r3_s.at[1], i)

    owner = me < OWNERS

    @pl.when(owner)
    def _():
        came_all(ar1.at[pl.ds(0, CTX - 1)], r1_s.at[1])
        ar1[me] = part[:, cols(me)]
        sum1[...] = jnp.sum(ar1[...], axis=0)
        loop(0, DPS - 1, lambda i: dp_out(i).start())

    steps_z = dot(zhi[...], onehot[...]) + dot(zlo[...], onehot[...])
    e = jnp.exp(-jnp.abs(raw))
    gate = jnp.where(raw >= 0, 1.0, e) / (1.0 + e)
    sg_ref[...] = steps_z.T[0:HEADS, :] * gate

    grad_halo.wait_recv()
    gp[TOK:, :] = jnp.where(me < CTX - 1, gp[TOK:, :], 0.0)

    def input_grad(j):
        c = cols(j)
        total = w_ref[0:1, c] * gp[3 : 3 + TOK, c]
        for k in range(1, TAPS):
            total = total + w_ref[k : k + 1, c] * gp[3 - k : 3 - k + TOK, c]
        gin_ref[:, c] = total.astype(BF16)

    loop(0, CH // 256, input_grad)

    @pl.when(owner)
    def _():
        came_all(ar2.at[pl.ds(0, DPS - 1)], r2_s.at[1])
        ar2[zed] = sum1[...]
        tot[:, cols(me)] = jnp.sum(ar2[...], axis=0)
        loop(0, CTX - 1, lambda i: total_out(far_first(i)).start())

    loop(CH // 256, CH // 128, input_grad)

    halo_copy.wait_send()
    grad_halo.wait_send()

    left_all(decg.at[pl.ds(0, CHIPS - 1)], dg_s.at[0])
    for k in range(2):
        left_all(tsum.at[k], p1_s.at[k])
        left_all(tsum.at[k], p2_s.at[k])
        left_all(rcv.at[k, pl.ds(0, CHIPS - 1)], a_s.at[k])
        left_all(rcv.at[k, pl.ds(0, CHIPS - 1)], b_s.at[k])

    @pl.when(owner)
    def _():
        some = tot.at[:, pl.ds(0, CH - 128)]
        left_all(some, r1_s.at[0])
        left_all(ar2.at[pl.ds(0, DPS - 1)], r2_s.at[0])
        left_all(ar1.at[pl.ds(0, CTX - 1)], r3_s.at[0])
        came_all(some, r3_s.at[1])

    @pl.when(jnp.logical_not(owner))
    def _():
        left_all(tot, r1_s.at[0])
        came_all(tot, r3_s.at[1])

    wg_ref[...] = tot[0:TAPS, :]
    for j in range(OWNERS):
        bg_ref[j : j + 1, :] = tot[4:5, 128 * j : 128 * j + 128]
    kg_ref[...] = tot[5:6, 0:HEADS]


def copy_kernel(*refs):
    n = len(refs) // 2
    copies = [pltpu.make_async_copy(refs[i], refs[n + i], refs[-1].at[i]) for i in range(n)]
    for copy in copies:
        copy.start()
    for copy in copies:
        copy.wait()


def scratch():
    v = pltpu.VMEM
    dma = pltpu.SemaphoreType.DMA
    return [
        v((TOK, CH), BF16),
        v((TOK, SIG), BF16),
        v((TAPS, CH), F32),
        v((OWNERS, 128), F32),
        v((1, HEADS), F32),
        v((HEADS, TOK), F32),
        v((TOK + 8, CH), F32),
        v((16, CH), BF16),
        v((TOK, CH), BF16),
        v((TOK, CH), F32),
        v((128, TOK), F32),
        v((128, TOK), F32),
        v((128, TOK), F32),
        v((TOK, HEADS * 128), F32),
        v((TOK, SIG), F32),
        v((TOK, SIG), F32),
        v((TOK, SIG), F32),
        v((TOK, SIG), BF16),
        v((TOK, SIG), BF16),
        v((TOK, SIG), BF16),
        v((2, STATE, SIG), BF16),
        v((2, HALF, SIG), BF16),
        v((8, 128), F32),
        v((8, 128), F32),
        v((CHIPS, 8, 128), F32),
        v((CHIPS, SIG), F32),
        v((8, SIG), F32),
        v((1, SIG), F32),
        v((2, HALF, SIG), BF16),
        v((2, CHIPS, ROWS, GW), BF16),
        v((2, CHIPS, ROWS, GW), BF16),
        v((2, HALF, SIG), BF16),
        v((2, HALF, SIG), BF16),
        v((2, STATE, SIG), BF16),
        v((TOK, SIG), F32),
        v((TOK, SIG), F32),
        v((TOK, 128), F32),
        v((TOK, GW), F32),
        v((TAPS - 1, TOK, CH), F32),
        v((TOK + 8, CH), F32),
        v((TOK, SIG), BF16),
        v((TOK, SIG), BF16),
        v((SIG, 128), BF16),
        v((8, SIG), F32),
        v((8, CH), F32),
        v((CTX, 8, 128), F32),
        v((DPS, 8, 128), F32),
        v((8, 128), F32),
        v((8, CH), F32),
        dma((7,)),
        dma((2,)),
        dma((2,)),
        dma((2,)),
        dma((2,)),
        dma((2, GROUPS)),
        dma((2,)),
        dma((2,)),
        dma((2,)),
        dma((2, GROUPS)),
        dma((2,)),
        dma((2, GROUPS)),
        dma((2,)),
        dma((2,)),
        dma((2,)),
        dma((2,)),
    ]


def body(conv_input, step_raw, log_decay, cotangent, conv_weight, conv_bias, skip_gain):
    vmem = pl.BlockSpec(memory_space=pltpu.VMEM)
    hbm = pl.BlockSpec(memory_space=pltpu.HBM)
    shapes = (
        jax.ShapeDtypeStruct((TOK, SIG), BF16),
        jax.ShapeDtypeStruct((TOK, CH), BF16),
        jax.ShapeDtypeStruct((HEADS, TOK), F32),
        jax.ShapeDtypeStruct((TAPS, CH), F32),
        jax.ShapeDtypeStruct((OWNERS, 128), F32),
        jax.ShapeDtypeStruct((1, HEADS), F32),
    )
    results = pl.pallas_call(
        kernel,
        out_shape=[pltpu.VMEM(a.shape, a.dtype) for a in shapes],
        in_specs=[hbm] * 7,
        out_specs=[vmem] * 6,
        scratch_shapes=scratch(),
        compiler_params=pltpu.CompilerParams(
            collective_id=0, has_side_effects=True, vmem_limit_bytes=VMEM
        ),
    )(*(pltpu.with_memory_space_constraint(a, pltpu.HBM) for a in (
        conv_input[0], step_raw[0].T, log_decay[0].T, cotangent[0],
        conv_weight, conv_bias.reshape(OWNERS, 128), skip_gain[None],
    )))
    out, gin, sg, wg, bg, kg = pl.pallas_call(
        copy_kernel,
        out_shape=shapes,
        in_specs=[vmem] * 6,
        out_specs=[hbm] * 6,
        scratch_shapes=[pltpu.SemaphoreType.DMA((6,))],
    )(*(pltpu.with_memory_space_constraint(a, pltpu.VMEM) for a in results))
    return out[None], gin[None], sg.T[None], wg, bg.reshape(CH), kg[0]


def solution(mesh):
    split = P("dp", "ctx", None)
    return jax.shard_map(
        body,
        mesh=mesh,
        in_specs=(split, split, split, split, P(), P(), P()),
        out_specs=(split, split, split, P(), P(), P()),
        check_vma=False,
    )
```
